32 devices in a mesh: sec: 4 (over y, x), tile: 2 (over core), lev: 4 (over z).
Axes of the slice: x: 2, y: 2, z: 4, core: 2. Of those that a mesh axis runs over, the one named last changes fastest.
Arguments:
- ocean_conc: float32 [8, 256, 512], P('lev', ('sec', 'tile')), may hold values from 0.1 to 2.9
- flow_lo: bfloat16 [256, 512], P(('sec', 'tile')), as said below
- flow_hi: bfloat16 [256, 512], P(('sec', 'tile')), as said below
- flow_y: bfloat16 [256, 512], P(('sec', 'tile')), as said below
- open_lo: int32 [256, 512], P(('sec', 'tile')), may hold values from 0 to 1, as said below
- open_hi: int32 [256, 512], P(('sec', 'tile')), may hold values from 0 to 1
- open_y: int32 [256, 512], P(('sec', 'tile')), may hold values from 0 to 1, as said below
- settle_rate: float32 [8], P('lev'), may hold values from 0.01 to 0.1
- critical_stress: float32 [8], P('lev'), may hold values from 0.05 to 0.5
- erosion_rate: float32 [8], P('lev'), may hold values from 0.002 to 0.02
- wave_energy: bfloat16 [768, 4096], P('lev', ('sec', 'tile')), may hold values from 0 to 2
- band_angle: float32 [768], P('lev'), may hold values from -3.140625 to 3.140625
- band_speed: float32 [768], P('lev'), may hold values from 0.2 to 0.3
- band_growth: float32 [768], P('lev'), may hold values from 0.05 to 0.5
- band_orbital: float32 [768], P('lev'), may hold values from 0.01 to 0.1
- neighbors: int32 [4, 4096], P(None, ('sec', 'tile')), may hold values from 0 to 4095, as said below
- facing_angle: float32 [4, 4096], P(None, ('sec', 'tile')), may hold values from -3.140625 to 3.140625
- live_nodes: int32 [4096], P(('sec', 'tile')), may hold values 0 or 1
- remap_owner: int32 [512, 1], P(('sec', 'tile')), may hold values from 0 to 7; in each aligned block of 64 rows (0 to 63, 64 to 127, ...) at most 16 rows name the same one
- remap_slot: int32 [512], P(('sec', 'tile')), may hold values from 0 to 7
- remap_cell: int32 [512], P(('sec', 'tile')), may hold values from 0 to 255
- remap_weight: bfloat16 [512, 64, 64], P(('sec', 'tile')), may hold values from -0.25 to 0.25
Outputs:
- sediment_out: float32 [8, 256, 512], P('lev', ('sec', 'tile'))
- waves_out: bfloat16 [768, 4096], P('lev', ('sec', 'tile'))
The draws below stay inside these ranges and needn't reach their ends.
Inputs may be any that keep to these rules, and one draw needn't show every extreme that they name: open_hi of row r equals open_lo of row r + 1; the lower face of the first row and the upper face of the last row are closed. `open_y`: the face after the last column is closed. flow_lo is zero where open_lo is 0, of magnitude at most 0.150390625; flow_hi of row r equals flow_lo of row r + 1. `flow_hi`: zero where open_hi is 0, of magnitude at most 0.150390625. `flow_y`: zero where open_y is 0, of magnitude at most 0.150390625. `neighbors`: each neighbour's index differs from its node's index by at most 128. `remap_owner`: among the 64 entries of one device at most 16 name the same owner.
All inputs are finite; a program needn't handle non-finite values. No bound on the sum of `live_nodes` on one device may be relied on, other than what follows from the above.
Results may differ from the reference program's by a relative error of at most 0.001.
Values sent between devices are 32-bit elements; how exact they have to be, the bound alone decides.
A program may use at most 64 MiB of HBM per device.

```python
import math
import jax
import jax.numpy as jnp
import numpy as np
from jax import lax

OY = 512
OSTEPS = 4
BANDS = 768
WSTEPS = 4
NBRS = 4
ENT = 64
PEERS = 8
CLASSES = 8
OX = 256
OB_DEV = 256
WNODES = 4096
WB_DEV = 8
CAP = 16


def open_faces_x(key):
    interior = (jax.random.randint(jax.random.fold_in(key, 101), (OX - 1, OY), 0, 8) < 7).astype(jnp.int32)
    closed = jnp.zeros((1, OY), jnp.int32)
    return jnp.concatenate([closed, interior, closed], axis=0)


def open_faces_y(key):
    interior = (jax.random.randint(jax.random.fold_in(key, 102), (OX, OY - 1), 0, 8) < 7).astype(jnp.int32)
    return jnp.concatenate([interior, jnp.zeros((OX, 1), jnp.int32)], axis=1)


def face_speed(key, extent):
    return jax.random.uniform(key, extent, jnp.float32, -0.15, 0.15)


def current_speed_x(key, extent):
    column_sign = jnp.where(jax.random.uniform(jax.random.fold_in(key, 3), (1, extent[1]), jnp.float32) < 0.5, -1.0, 1.0)
    magnitude = jax.random.uniform(jax.random.fold_in(key, 1), extent, jnp.float32, 0.65, 1.0)
    return 0.15 * magnitude * column_sign


def faces_x_flow(key):
    return current_speed_x(jax.random.fold_in(key, 103), (OX + 1, OY)) * open_faces_x(key).astype(jnp.float32)


def draw_flow_lo(key, part):
    return faces_x_flow(key)[:-1].astype(jnp.bfloat16)


def draw_flow_hi(key, part):
    return faces_x_flow(key)[1:].astype(jnp.bfloat16)


def draw_flow_y(key, part):
    speed_field = face_speed(jax.random.fold_in(key, 104), (OX, OY)) * open_faces_y(key).astype(jnp.float32)
    return speed_field.astype(jnp.bfloat16)


def draw_open_lo(key, part):
    return open_faces_x(key)[:-1]


def draw_open_hi(key, part):
    return open_faces_x(key)[1:]


def draw_open_y(key, part):
    return open_faces_y(key)


def draw_neighbors(key, part):
    nodes = jnp.arange(WNODES, dtype=jnp.int32)
    far_reach = jax.random.randint(jax.random.fold_in(key, 105), (2, WNODES), 96, 129)
    far_reach = jnp.where((nodes % 64 == 0)[None, :], 128, far_reach)
    near_reach = jax.random.randint(jax.random.fold_in(key, 106), (2, WNODES), -128, 129)
    offsets = jnp.concatenate([-far_reach[0:1], far_reach[1:2], near_reach], axis=0)
    return jnp.clip(nodes[None, :] + offsets, 0, WNODES - 1).astype(jnp.int32)


def place_ends(values, rng, least, top_value):
    longest = values.shape.index(max(values.shape))
    spots = []
    for shift in (0, 1):
        where = [jax.random.randint(jax.random.fold_in(rng, axis), (), 0, length) for axis, length in enumerate(values.shape)]
        where[longest] = (where[longest] + shift) % values.shape[longest]
        spots.append(tuple(where))
    return values.at[spots[0]].set(least).at[spots[1]].set(top_value)


def block_levels(own_key, dims, split, least, high):
    loudness, own = 1.0, jax.random.fold_in(own_key, 6)
    for axis_at, shards_of in split:
        heights = jnp.exp(jax.random.uniform(jax.random.fold_in(own, axis_at), (shards_of,), jnp.float32, least / len(split), high / len(split)))
        loudness = loudness * jnp.repeat(heights, dims[axis_at] // shards_of).reshape([-1 if axis == axis_at else 1 for axis in range(len(dims))])
    return loudness


def shared_out(rng, own, number, rows, number_of, top, reach, lean):
    ranking = jax.random.permutation(rng, number_of)
    heavy_load, common = portions_of(number_of, rows * top, reach, lean, True), portions_of(number_of, rows * top, reach, lean, False)
    places = jnp.arange(number_of)

    def named(lengths, offset_by):
        used = int((lengths > 0).sum())
        fixed = max(1, used // 4)
        moved = fixed + (places - fixed + offset_by * (used - fixed)) % max(1, number_of - fixed)
        return jnp.zeros((number_of,), jnp.int32).at[ranking[jnp.where(places < fixed, places, moved)]].set(jnp.asarray(lengths, jnp.int32))

    lengths = jnp.where(number % 4 == 0, named(heavy_load, number // 4), named(common, number - number // 4 - 1))
    mixed = jax.random.permutation(jax.random.fold_in(own, 3), number_of)
    donor, sink = mixed[0:number_of // 2 * 2:2], mixed[1:number_of // 2 * 2:2]
    slack = jnp.minimum(lengths[donor] - 1, reach - lengths[sink]) // 2
    slack = jnp.where((donor == ranking[0]) | (sink == ranking[0]) | (lengths[sink] == 0), 0, jnp.maximum(slack, 0))
    moved = jax.random.randint(jax.random.fold_in(own, 4), (number_of // 2,), 0, 1 << 20) % (slack + 1)
    lengths = lengths.at[donor].add(-moved).at[sink].add(moved)
    members = jnp.searchsorted(jnp.cumsum(lengths), jnp.arange(rows * top), side="right").astype(jnp.int32)
    listing = members.reshape(top, rows).T
    listing = listing[jax.random.permutation(jax.random.fold_in(own, 1), rows)]
    offset_by = jax.random.randint(jax.random.fold_in(own, 2), (rows, 1), 0, top)
    return jnp.take_along_axis(listing, (jnp.arange(top)[None, :] + offset_by) % top, axis=1)


def portions_of(amount, total, most, lean, full):
    portions = [(1 << 20) // math.isqrt(standing ** lean) + 1 for standing in range(1, amount + 1)]
    largest = most if full else min(most, max(-(-total // amount), total * portions[0] // sum(portions)))
    least = 1 if total - largest >= amount - 1 else 0
    given, spare = [largest] + [least] * (amount - 1), total - largest - least * (amount - 1)
    while spare > 0:
        candidates = [i for i in range(1, amount) if given[i] < largest] or [i for i in range(1, amount) if given[i] < most]
        pool, left = sum([portions[i] for i in candidates]), spare
        for i in candidates:
            extra = min(most - given[i], max(1, left * portions[i] // pool), spare)
            given[i] = given[i] + extra
            spare = spare - extra
    return np.array(given)


def scatter_about(key, dims, scale, limit, split=(), kind=jnp.bfloat16):
    result = scale * jax.random.normal(key, dims, jnp.float32)
    if split:
        result = result * block_levels(key, dims, split, -0.22, 0.18)
    return jnp.clip(result, -limit, limit).astype(kind)


def setup_inputs(seed: int = 0) -> dict:
    arg_keys = jax.random.split(jax.random.key(seed), 23)
    ocean_conc = jnp.clip(0.1 + 2.8000001 * jax.random.uniform(arg_keys[0], (CLASSES, OX, OY), jnp.float32) ** block_levels(arg_keys[0], (CLASSES, OX, OY), ((0, 4), (1, 8)), -0.2, 0.2), 0.1, 2.9)
    flow_lo = draw_flow_lo(jax.random.fold_in(arg_keys[22], 71), 0)
    flow_hi = draw_flow_hi(jax.random.fold_in(arg_keys[22], 71), 0)
    flow_y = draw_flow_y(jax.random.fold_in(arg_keys[22], 71), 0)
    open_lo = draw_open_lo(jax.random.fold_in(arg_keys[22], 71), 0)
    open_hi = draw_open_hi(jax.random.fold_in(arg_keys[22], 71), 0)
    open_y = draw_open_y(jax.random.fold_in(arg_keys[22], 71), 0)
    settle_rate = jnp.clip(jnp.exp(math.log(0.1) - 2.3025851 * jax.random.uniform(arg_keys[7], (CLASSES,), jnp.float32) ** block_levels(arg_keys[7], (CLASSES,), ((0, 4),), -0.2, 0.2)), 0.01, 0.1)
    critical_stress = jnp.clip(jnp.exp(math.log(0.5) - 2.3025851 * jax.random.uniform(arg_keys[8], (CLASSES,), jnp.float32) ** block_levels(arg_keys[8], (CLASSES,), ((0, 4),), -0.2, 0.2)), 0.05, 0.5)
    erosion_rate = jnp.clip(jnp.exp(math.log(0.02) - 2.30258502 * jax.random.uniform(arg_keys[9], (CLASSES,), jnp.float32) ** block_levels(arg_keys[9], (CLASSES,), ((0, 4),), -0.2, 0.2)), 0.002, 0.02)
    wave_energy = jnp.clip(2.0 * jax.random.uniform(arg_keys[10], (BANDS, WNODES), jnp.float32) ** block_levels(arg_keys[10], (BANDS, WNODES), ((0, 4), (1, 8)), -0.2, 0.2), 0.0, 2.0).astype(jnp.bfloat16)
    band_angle = jnp.clip(jax.random.uniform(arg_keys[11], (BANDS,), jnp.float32, -3.140625, 3.140625), -3.140625, 3.140625)
    band_speed = jnp.clip(0.2 + 0.10000001 * jax.random.uniform(arg_keys[12], (BANDS,), jnp.float32) ** block_levels(arg_keys[12], (BANDS,), ((0, 4),), -0.2, 0.2), 0.2, 0.3)
    band_growth = jnp.clip(jnp.exp(math.log(0.5) - 2.3025851 * jax.random.uniform(arg_keys[13], (BANDS,), jnp.float32) ** block_levels(arg_keys[13], (BANDS,), ((0, 4),), -0.2, 0.2)), 0.05, 0.5)
    band_orbital = jnp.clip(jnp.exp(math.log(0.1) - 2.3025851 * jax.random.uniform(arg_keys[14], (BANDS,), jnp.float32) ** block_levels(arg_keys[14], (BANDS,), ((0, 4),), -0.2, 0.2)), 0.01, 0.1)
    neighbors = draw_neighbors(jax.random.fold_in(arg_keys[22], 71), 0)
    facing_angle = jnp.clip(jax.random.uniform(arg_keys[16], (NBRS, WNODES), jnp.float32, -3.140625, 3.140625), -3.140625, 3.140625)
    live_nodes = place_ends((jax.random.randint(arg_keys[17], (WNODES,), 0, 8) < 7).astype(jnp.int32), jax.random.fold_in(arg_keys[17], 1), 0, 1)
    remap_owner_keys = jax.random.split(jax.random.fold_in(arg_keys[18], 1), (PEERS * ENT) // ENT)
    remap_owner_turns = jax.random.permutation(jax.random.fold_in(arg_keys[18], 3), (PEERS * ENT) // ENT)
    remap_owner = jax.vmap(lambda own, number: shared_out(jax.random.fold_in(arg_keys[18], 2), own, number, ENT, PEERS, 1, CAP, 2))(remap_owner_keys, remap_owner_turns).reshape((PEERS * ENT, 1))
    remap_slot = place_ends(jax.random.randint(arg_keys[19], (PEERS * ENT,), 0, WB_DEV), jax.random.fold_in(arg_keys[19], 1), 0, WB_DEV - 1).astype(jnp.int32)
    remap_cell = place_ends(jax.random.randint(arg_keys[20], (PEERS * ENT,), 0, OB_DEV), jax.random.fold_in(arg_keys[20], 1), 0, OB_DEV - 1).astype(jnp.int32)
    remap_weight = scatter_about(arg_keys[21], (PEERS * ENT, 64, 64), (64 * ENT // WB_DEV) ** -0.5, 0.25, ((0, 8),))
    return {"ocean_conc": ocean_conc, "flow_lo": flow_lo, "flow_hi": flow_hi, "flow_y": flow_y, "open_lo": open_lo, "open_hi": open_hi, "open_y": open_y, "settle_rate": settle_rate, "critical_stress": critical_stress, "erosion_rate": erosion_rate, "wave_energy": wave_energy, "band_angle": band_angle, "band_speed": band_speed, "band_growth": band_growth, "band_orbital": band_orbital, "neighbors": neighbors, "facing_angle": facing_angle, "live_nodes": live_nodes, "remap_owner": remap_owner, "remap_slot": remap_slot, "remap_cell": remap_cell, "remap_weight": remap_weight}


KAPPA = 0.07
FORCE_SCALE = 5.0
DRAG = 50.0
TAU_CURRENT = 20.0
TAU_WAVES = 10.0
HIGHEST = lax.Precision.HIGHEST

def coupling_fields(flow_lo, flow_hi, flow_y):
    eastward = 0.5 * (flow_lo.astype(jnp.float32) + flow_hi.astype(jnp.float32))
    across = flow_y.astype(jnp.float32)
    earlier = jnp.pad(across, ((0, 0), (1, 0)))[:, :-1]
    northward = 0.5 * (across + earlier)
    current_speed = jnp.sqrt(eastward * eastward + northward * northward)
    forcing = jnp.stack([FORCE_SCALE * eastward, FORCE_SCALE * northward, DRAG * current_speed * eastward, DRAG * current_speed * northward])
    return (forcing, eastward * eastward + northward * northward)

def band_rates(wave_forcing, band_dir, band_pace, growth, facing):
    cosines = jnp.cos(band_dir)[:, None]
    sine_terms = jnp.sin(band_dir)[:, None]
    drift_term = cosines * wave_forcing[0][None, :] + sine_terms * wave_forcing[1][None, :]
    push_term = jnp.maximum(cosines * wave_forcing[2][None, :] + sine_terms * wave_forcing[3][None, :], 0.0)
    base_rate = 0.5 * band_pace[:, None] * (1.0 + 0.5 * jnp.tanh(drift_term))
    inflow = base_rate[None] * jnp.maximum(-jnp.cos(band_dir[None, :, None] - facing[:, None, :]), 0.0)
    return (growth[:, None] * push_term, inflow)

def ocean_step(sediment, above_rows, below_rows, flow_lo, flow_hi, flow_y, open_lo, open_hi, open_y, settle_rate, erosion_gain):
    right_cells = jnp.pad(sediment, ((0, 0), (0, 0), (0, 1)))[:, :, 1:]
    flux_lo = jnp.maximum(flow_lo, 0.0) * above_rows + jnp.minimum(flow_lo, 0.0) * sediment - KAPPA * open_lo * (sediment - above_rows)
    flux_hi = jnp.maximum(flow_hi, 0.0) * sediment + jnp.minimum(flow_hi, 0.0) * below_rows - KAPPA * open_hi * (below_rows - sediment)
    flux_y = jnp.maximum(flow_y, 0.0) * sediment + jnp.minimum(flow_y, 0.0) * right_cells - KAPPA * open_y * (right_cells - sediment)
    flux_left = jnp.pad(flux_y, ((0, 0), (0, 0), (1, 0)))[:, :, :-1]
    return sediment - (flux_hi - flux_lo) - (flux_y - flux_left) - settle_rate[:, None, None] * sediment + erosion_gain

def reference(ocean_conc, flow_lo, flow_hi, flow_y, open_lo, open_hi, open_y, settle_rate, critical_stress, erosion_rate, wave_energy, band_angle, band_speed, band_growth, band_orbital, neighbors, facing_angle, live_nodes, remap_owner, remap_slot, remap_cell, remap_weight):
    forcing, current_square = coupling_fields(flow_lo, flow_hi, flow_y)
    entry_count = PEERS * ENT
    source = jnp.arange(entry_count, dtype=jnp.int32) // ENT * OB_DEV + remap_cell
    target = remap_owner[:, 0] * WB_DEV + remap_slot
    weights = remap_weight.astype(jnp.float32)
    picked = jnp.transpose(forcing.reshape(4, PEERS * OB_DEV, 64)[:, source, :], (1, 0, 2))
    pieces = jnp.einsum('eji,eci->ecj', weights, picked, precision=HIGHEST).reshape(entry_count, 256)
    wave_blocks = jax.ops.segment_sum(pieces, target, num_segments=PEERS * WB_DEV)
    wave_forcing = jnp.transpose(wave_blocks.reshape(PEERS * WB_DEV, 4, 64), (1, 0, 2)).reshape(4, WNODES)
    alive_mask = live_nodes.astype(jnp.float32)[None, :]
    band_group = math.gcd(BANDS, 32)

    def wave_group(orbital, inputs):
        energy_in, band_dir, band_pace, growth, orbit_gain = inputs
        source_term, inflow = band_rates(wave_forcing, band_dir, band_pace, growth, facing_angle)
        total_rate = lax.optimization_barrier(jnp.sum(inflow, axis=0))
        energy = (energy_in.astype(jnp.float32) + source_term) * alive_mask
        for sweep in range(WSTEPS):
            arriving = jnp.zeros_like(energy)
            for neighbor in range(NBRS):
                arriving = arriving + inflow[neighbor] * energy[:, neighbors[neighbor]]
            energy = (energy + arriving - total_rate * energy) * alive_mask
        coefficient = jnp.stack([orbit_gain * jnp.cos(band_dir), orbit_gain * jnp.sin(band_dir)])
        orbital = orbital + jnp.dot(coefficient, energy, precision=HIGHEST)
        return (orbital, energy.astype(jnp.bfloat16))
    grouped = (wave_energy.reshape(BANDS // band_group, band_group, WNODES), band_angle.reshape(-1, band_group), band_speed.reshape(-1, band_group), band_growth.reshape(-1, band_group), band_orbital.reshape(-1, band_group))
    orbital, wave_rows = lax.scan(wave_group, jnp.zeros((2, WNODES), jnp.float32), grouped)
    waves_out = wave_rows.reshape(BANDS, WNODES)
    orbital_blocks = jnp.transpose(orbital.reshape(2, PEERS * WB_DEV, 64), (1, 0, 2))
    returned = orbital_blocks[target]
    spread = jnp.einsum('eji,ecj->eci', weights, returned, precision=HIGHEST).reshape(entry_count, 128)
    ocean_blocks = jax.ops.segment_sum(spread, source, num_segments=PEERS * OB_DEV)
    ocean_orbital = jnp.transpose(ocean_blocks.reshape(PEERS * OB_DEV, 2, 64), (1, 0, 2)).reshape(2, OX, OY)
    stress = TAU_CURRENT * current_square + TAU_WAVES * (ocean_orbital[0] * ocean_orbital[0] + ocean_orbital[1] * ocean_orbital[1])
    erosion_gain = erosion_rate[:, None, None] * jnp.maximum(stress[None] / critical_stress[:, None, None] - 1.0, 0.0)
    lower_flow = flow_lo.astype(jnp.float32)
    upper_flow = flow_hi.astype(jnp.float32)
    side_flow = flow_y.astype(jnp.float32)
    lower_open = open_lo.astype(jnp.float32)
    upper_open = open_hi.astype(jnp.float32)
    side_open = open_y.astype(jnp.float32)
    sediment = ocean_conc
    for sweep in range(OSTEPS):
        above_rows = jnp.pad(sediment, ((0, 0), (1, 0), (0, 0)))[:, :-1]
        below_rows = jnp.pad(sediment, ((0, 0), (0, 1), (0, 0)))[:, 1:]
        sediment = ocean_step(sediment, above_rows, below_rows, lower_flow, upper_flow, side_flow, lower_open, upper_open, side_open, settle_rate, erosion_gain)
    return (sediment, waves_out)
```

```python
import functools

import jax
import jax.numpy as jnp
from jax import lax
from jax.experimental import pallas as pl
from jax.experimental.pallas import tpu as pltpu
from jax.sharding import PartitionSpec as P

OSTEPS = 4
WSTEPS = 4
NBRS = 4
KAPPA = 0.07
FORCE_SCALE = 5.0
DRAG = 50.0
TAU_CURRENT = 20.0
TAU_WAVES = 10.0
MESH = pl.DeviceIdType.MESH
F32 = jnp.float32
BF16 = jnp.bfloat16


def parts(x):
    hi = x.astype(BF16)
    lo = (x - hi.astype(F32)).astype(BF16)
    return hi, lo


def two(x, axis):
    return jnp.concatenate(parts(x), axis=axis)


def dot(a, b):
    return jnp.dot(a, b, preferred_element_type=F32)


def fold(x):
    total = x[:, 0:128]
    for i in range(1, x.shape[1] // 128):
        total = total + x[:, 128 * i : 128 * i + 128]
    return total + pltpu.roll(total, 64, axis=1)


def iota(shape, dim):
    return lax.broadcasted_iota(jnp.int32, shape, dim)


def kernel(
    sizes,
    conc, flow_lo, flow_hi, flow_y, open_lo, open_hi, open_y,
    settle, critical, erosion,
    wave, bands, meta_in, ent_cols, ent_rows, weight,
    sed_out, wave_out,
    we, meta, conc_x, fields, tau_x, table, table_in, wf,
    select, inflow, keep, energy, split, orb, orb_in, gathered,
    halo_send, halo_recv, table_send, table_recv, lev_send, lev_recv, orb_send, orb_recv,
):
    n_tile, n, n_lev = sizes
    bins = wave.shape[0]
    rows, cols = flow_lo.shape
    ent = ent_cols.shape[0]
    pairs = 4 * n
    classes = conc.shape[0]
    sec, tile, lev = lax.axis_index("sec"), lax.axis_index("tile"), lax.axis_index("lev")
    me = sec * n_tile + tile

    def plane(peer):
        return {"sec": peer // n_tile, "tile": lax.rem(peer, n_tile)}

    barrier = pltpu.get_barrier_semaphore()

    @pl.loop(1, n)
    def _(off):
        pl.semaphore_signal(
            barrier, inc=1, device_id=plane(lax.rem(me + off, n)), device_id_type=MESH
        )

    @pl.loop(1, n_lev)
    def _(off):
        pl.semaphore_signal(
            barrier, inc=1, device_id={"lev": lax.rem(lev + off, n_lev)}, device_id_type=MESH
        )

    for j in range(4):
        we[4 + j] = wave[:, 128 * j : 128 * j + 128].astype(F32)
        meta[4 + j] = meta_in[:, 128 * j : 128 * j + 128]

    lo, hi, side = flow_lo[...].astype(F32), flow_hi[...].astype(F32), flow_y[...].astype(F32)
    ol, oh, oy = open_lo[...].astype(F32), open_hi[...].astype(F32), open_y[...].astype(F32)
    first_col = iota((rows, cols), 1) == 0

    def left_of(x):
        return jnp.where(first_col, 0.0, pltpu.roll(x, 1, axis=1))

    east = 0.5 * (lo + hi)
    north = 0.5 * (side + left_of(side))
    square = east * east + north * north
    speed = jnp.sqrt(square)
    a_y = jnp.maximum(side, 0.0) + KAPPA * oy
    b_y = jnp.minimum(side, 0.0) - KAPPA * oy
    a_hi = jnp.maximum(hi, 0.0) + KAPPA * oh
    b_hi = jnp.minimum(hi, 0.0) - KAPPA * oh
    a_lo = jnp.maximum(lo, 0.0) + KAPPA * ol
    b_lo = jnp.minimum(lo, 0.0) - KAPPA * ol
    mid = pl.ds(8, rows)
    fields[0, mid] = 1.0 - a_hi + b_lo - a_y + left_of(b_y)
    fields[1, mid] = a_lo
    fields[2, mid] = -b_hi
    fields[3, mid] = -b_y
    fields[4, mid] = left_of(a_y)
    fields[5, mid] = TAU_CURRENT * square
    for c in range(classes):
        conc_x[c, mid] = conc[c]

    @pl.when(me == 0)
    def _():
        we[0:4] = jnp.zeros((4, bins, 128), F32)
        meta[0:4] = jnp.zeros((4, 16, 128), F32)
        fields[:, 0:8] = jnp.zeros((6, 8, cols), F32)
        conc_x[:, 0:8] = jnp.zeros((classes, 8, cols), F32)
        tau_x[0:8] = jnp.zeros((8, cols), F32)

    @pl.when(me == n - 1)
    def _():
        we[8:12] = jnp.zeros((4, bins, 128), F32)
        meta[8:12] = jnp.zeros((4, 16, 128), F32)
        fields[:, rows + 8 : rows + 16] = jnp.zeros((6, 8, cols), F32)
        conc_x[:, rows + 8 : rows + 16] = jnp.zeros((classes, 8, cols), F32)
        tau_x[rows + 8 : rows + 16] = jnp.zeros((8, cols), F32)

    pl.semaphore_wait(barrier, n - 1 + n_lev - 1)

    def to_right(src, dst, i):
        return pltpu.make_async_remote_copy(
            src_ref=src, dst_ref=dst,
            send_sem=halo_send.at[0, i], recv_sem=halo_recv.at[0, i],
            device_id=plane(lax.rem(me + 1, n)), device_id_type=MESH,
        )

    def to_left(src, dst, i):
        return pltpu.make_async_remote_copy(
            src_ref=src, dst_ref=dst,
            send_sem=halo_send.at[1, i], recv_sem=halo_recv.at[1, i],
            device_id=plane(lax.rem(me + n - 1, n)), device_id_type=MESH,
        )

    own, before, after = pl.ds(4, 4), pl.ds(0, 4), pl.ds(8, 4)
    top, bottom = pl.ds(8, 8), pl.ds(rows, 8)
    above, below = pl.ds(0, 8), pl.ds(rows + 8, 8)
    right = [
        to_right(meta.at[own], meta.at[before], 0),
        to_right(we.at[own], we.at[before], 1),
        to_right(fields.at[:, bottom], fields.at[:, above], 2),
        to_right(conc_x.at[:, bottom], conc_x.at[:, above], 3),
        to_right(tau_x.at[bottom], tau_x.at[above], 4),
    ]
    left = [
        to_left(meta.at[own], meta.at[after], 0),
        to_left(we.at[own], we.at[after], 1),
        to_left(fields.at[:, top], fields.at[:, below], 2),
        to_left(conc_x.at[:, top], conc_x.at[:, below], 3),
        to_left(tau_x.at[top], tau_x.at[below], 4),
    ]

    def start(items):
        @pl.when(me < n - 1)
        def _():
            for i in items:
                right[i].start()

        @pl.when(me > 0)
        def _():
            for i in items:
                left[i].start()

    def arrived(items):
        @pl.when(me > 0)
        def _():
            for i in items:
                right[i].wait_recv()

        @pl.when(me < n - 1)
        def _():
            for i in items:
                left[i].wait_recv()

    def sent(items):
        @pl.when(me < n - 1)
        def _():
            for i in items:
                right[i].wait_send()

        @pl.when(me > 0)
        def _():
            for i in items:
                left[i].wait_send()

    start([0, 1])

    cell_row, cell_col = ent_cols[:, 0:1], ent_cols[:, 1:2]
    pair_col, parity = ent_cols[:, 2:3], ent_cols[:, 3:4]
    row_hot = (iota((ent, rows), 1) == cell_row).astype(F32).astype(BF16)
    forcing = jnp.concatenate(
        [
            FORCE_SCALE * east,
            FORCE_SCALE * north,
            DRAG * speed * east,
            DRAG * speed * north,
        ],
        axis=1,
    )
    picked = dot(jnp.concatenate([row_hot, row_hot], axis=1), two(forcing, 0))
    cell_mask = (iota((ent, cols), 1) // 64 == cell_col).astype(F32)
    channels = [fold(picked[:, cols * c : cols * c + cols] * cell_mask)[:, 0:64] for c in range(4)]
    group_mask = (iota((32, 512), 1) // 64 == lax.rem(iota((32, 512), 0), 8)).astype(F32)
    pieces = []
    for g in range(ent // 8):
        left_side = two(jnp.concatenate([x[8 * g : 8 * g + 8] for x in channels], axis=0), 0)
        block = lax.dot_general(
            left_side, weight[512 * g : 512 * g + 512, :],
            (((1,), (1,)), ((), ())), preferred_element_type=F32,
        )
        pieces.append(fold((block[0:32] + block[32:64]) * group_mask))
    parity_mask = (iota((ent, 128), 1) // 64 == parity).astype(F32)
    stacked = jnp.concatenate(
        [
            jnp.concatenate([x[8 * c : 8 * c + 8] for x in pieces], axis=0) * parity_mask
            for c in range(4)
        ],
        axis=1,
    )
    pair_hot = (iota((pairs, ent), 0) == ent_rows[0:1, :]).astype(F32).astype(BF16)
    sums = dot(jnp.concatenate([pair_hot, pair_hot], axis=1), two(stacked, 0))
    table[0:4] = jnp.zeros((4, 4, 128), F32)
    table[pairs + 4 : pairs + 8] = jnp.zeros((4, 4, 128), F32)
    for c in range(4):
        table[4 : pairs + 4, c, :] = sums[:, 128 * c : 128 * c + 128]

    def table_copy(off):
        peer = lax.rem(me + off, n)
        return pltpu.make_async_remote_copy(
            src_ref=table.at[pl.ds(4 * peer, 12)], dst_ref=table_in.at[off],
            send_sem=table_send.at[off], recv_sem=table_recv.at[off],
            device_id=plane(peer), device_id_type=MESH,
        )

    @pl.loop(1, n)
    def _(off):
        table_copy(off).start()

    start([2, 3])

    arrived([0])

    @pl.loop(1, 11)
    def _(b):
        base = (4 * me - 5 + b) * 128
        near = meta[b][0:NBRS].astype(jnp.int32) - base
        for k in range(NBRS):
            hot = (iota((384, 128), 0) == near[k : k + 1, :]).astype(F32)
            select[b, :, 128 * k : 128 * k + 128] = hot.astype(BF16)

    arrived([1])
    wf[...] = table[pl.ds(4 * me, 12)]

    @pl.loop(1, n)
    def _(off):
        table_copy(off).wait_recv()
        wf[...] += table_in[off]

    cosine, sine = bands[:, 0:1], bands[:, 1:2]
    pace, growth = bands[:, 2:3], bands[:, 3:4]
    coef_c, coef_s = bands[:, 4:5], bands[:, 5:6]

    @pl.loop(0, 12)
    def _(b):
        w = wf[b]
        m = meta[b]
        alive = m[12:13, :]
        push = jnp.maximum(cosine * w[2:3, :] + sine * w[3:4, :], 0.0)
        first = (we[b] + growth * push) * alive
        energy[b] = first
        split[0, b] = two(first, 0)
        drift = cosine * w[0:1, :] + sine * w[1:2, :]
        rate = pace * (0.5 + 0.25 * jnp.tanh(drift)) * alive
        total = jnp.zeros((bins, 128), F32)
        for k in range(NBRS):
            flow = rate * jnp.maximum(
                -(cosine * m[4 + k : 5 + k, :] + sine * m[8 + k : 9 + k, :]), 0.0
            )
            inflow[b, k] = flow
            total = total + flow
        keep[b] = alive - total

    for step in range(WSTEPS):
        now, later = step % 2, (step + 1) % 2

        @pl.loop(step + 1, 11 - step)
        def _(b):
            window = jnp.concatenate(
                [split[now, b - 1], split[now, b], split[now, b + 1]], axis=1
            )
            got = dot(window, select[b])
            new = keep[b] * energy[b]
            for k in range(NBRS):
                lanes = slice(128 * k, 128 * k + 128)
                new = new + inflow[b, k] * (got[0:bins, lanes] + got[bins : 2 * bins, lanes])
            energy[b] = new
            if step < WSTEPS - 1:
                split[later, b] = two(new, 0)

    for j in range(4):
        final = energy[4 + j]
        orb[j, 0:1, :] = jnp.sum(coef_c * final, axis=0, keepdims=True)
        orb[j, 1:2, :] = jnp.sum(coef_s * final, axis=0, keepdims=True)

    def lev_copy(off):
        return pltpu.make_async_remote_copy(
            src_ref=orb, dst_ref=orb_in.at[off],
            send_sem=lev_send.at[off], recv_sem=lev_recv.at[off],
            device_id={"lev": lax.rem(lev + off, n_lev)}, device_id_type=MESH,
        )

    for off in range(1, n_lev):
        lev_copy(off).start()
    for j in range(4):
        wave_out[:, 128 * j : 128 * j + 128] = energy[4 + j].astype(BF16)
    full = orb[...]
    for off in range(1, n_lev):
        lev_copy(off).wait_recv()
        full = full + orb_in[off]
    mine = pl.ds(4 * me, 4)
    gathered[mine] = full

    def orb_copy(off):
        return pltpu.make_async_remote_copy(
            src_ref=gathered.at[mine], dst_ref=gathered.at[mine],
            send_sem=orb_send.at[off], recv_sem=orb_recv.at[off],
            device_id=plane(lax.rem(me + off, n)), device_id_type=MESH,
        )

    def orb_arrival(off):
        source = pl.ds(4 * lax.rem(me - off + n, n), 4)
        return pltpu.make_async_remote_copy(
            src_ref=gathered.at[mine], dst_ref=gathered.at[source],
            send_sem=orb_send.at[off], recv_sem=orb_recv.at[off],
            device_id=plane(lax.rem(me + off, n)), device_id_type=MESH,
        )

    @pl.loop(1, n)
    def _(off):
        orb_copy(off).start()

    hot = (iota((ent, pairs), 1) == pair_col).astype(F32).astype(BF16)
    group_mask = (iota((ent, 512), 1) // 64 == lax.rem(iota((ent, 512), 0), 8)).astype(F32)

    @pl.loop(1, n)
    def _(off):
        orb_arrival(off).wait_recv()

    field = jnp.concatenate([gathered[:, 0, :], gathered[:, 1, :]], axis=1)
    back = dot(jnp.concatenate([hot, hot], axis=1), two(field, 0))
    wide = []
    for c in range(2):
        x = fold(back[:, 128 * c : 128 * c + 128] * parity_mask)
        wide.append(jnp.concatenate([x, x, x, x], axis=1) * group_mask)
    spread = []
    for g in range(ent // 8):
        left_side = two(jnp.concatenate([x[8 * g : 8 * g + 8] for x in wide], axis=0), 0)
        block = dot(left_side, weight[512 * g : 512 * g + 512, :])
        spread.append(block[0:16] + block[16:32])
    row_hot_t = (iota((rows, ent), 0) == ent_rows[1:2, :]).astype(F32).astype(BF16)
    placed = []
    for c in range(2):
        x = jnp.concatenate([y[8 * c : 8 * c + 8] for y in spread], axis=0)
        placed.append(jnp.concatenate([x] * (cols // 64), axis=1) * cell_mask)
    orbital = dot(
        jnp.concatenate([row_hot_t, row_hot_t], axis=1), two(jnp.concatenate(placed, axis=1), 0)
    )
    orbital_c, orbital_s = orbital[:, 0:cols], orbital[:, cols : 2 * cols]
    tau_x[mid] = TAU_WAVES * (orbital_c * orbital_c + orbital_s * orbital_s)
    start([4])
    arrived([2, 3, 4])
    stress = fields[5] + tau_x[...]
    tall = rows + 16
    for c in range(classes):
        gain = erosion[c] * jnp.maximum(stress / critical[c] - 1.0, 0.0)
        centre = fields[0] - settle[c]
        state = conc_x[c]
        for _ in range(OSTEPS):
            state = (
                centre * state
                + fields[1] * pltpu.roll(state, 1, axis=0)
                + fields[2] * pltpu.roll(state, tall - 1, axis=0)
                + fields[3] * pltpu.roll(state, cols - 1, axis=1)
                + fields[4] * pltpu.roll(state, 1, axis=1)
                + gain
            )
        sed_out[c] = state[8 : rows + 8]

    sent([0, 1, 2, 3, 4])

    @pl.loop(1, n)
    def _(off):
        table_copy(off).wait_send()
        orb_copy(off).wait_send()

    for off in range(1, n_lev):
        lev_copy(off).wait_send()


def per_device(
    ocean_conc, flow_lo, flow_hi, flow_y, open_lo, open_hi, open_y,
    settle_rate, critical_stress, erosion_rate,
    wave_energy, band_angle, band_speed, band_growth, band_orbital,
    neighbors, facing_angle, live_nodes,
    remap_owner, remap_slot, remap_cell, remap_weight,
):
    n_tile = lax.axis_size("tile")
    n = lax.axis_size("sec") * n_tile
    n_lev = lax.axis_size("lev")
    rows, cols = flow_lo.shape
    bins, nodes = wave_energy.shape
    ent = remap_cell.shape[0]
    classes = ocean_conc.shape[0]
    pairs = 4 * n
    per_row = cols // 64
    cosine, sine = jnp.cos(band_angle), jnp.sin(band_angle)
    nothing = jnp.zeros_like(cosine)
    bands = jnp.stack(
        [cosine, sine, band_speed, band_growth, band_orbital * cosine, band_orbital * sine,
         nothing, nothing],
        axis=1,
    )
    meta = jnp.concatenate(
        [
            neighbors.astype(F32),
            jnp.cos(facing_angle),
            jnp.sin(facing_angle),
            live_nodes.astype(F32)[None],
            jnp.zeros((3, nodes), F32),
        ],
        axis=0,
    )
    owner = remap_owner[:, 0]
    pair = owner * 4 + remap_slot // 2
    ent_cols = jnp.stack(
        [remap_cell // per_row, remap_cell % per_row, pair, remap_slot % 2], axis=1
    )
    ent_rows = jnp.stack([pair, remap_cell // per_row], axis=0)
    vmem = pl.BlockSpec(memory_space=pltpu.VMEM)
    smem = pl.BlockSpec(memory_space=pltpu.SMEM)
    tall = rows + 16
    return pl.pallas_call(
        functools.partial(kernel, (n_tile, n, n_lev)),
        out_shape=(
            jax.ShapeDtypeStruct(ocean_conc.shape, F32),
            jax.ShapeDtypeStruct(wave_energy.shape, BF16),
        ),
        in_specs=[vmem] * 7 + [smem] * 3 + [vmem] * 6,
        out_specs=(vmem, vmem),
        scratch_shapes=[
            pltpu.VMEM((12, bins, 128), F32),
            pltpu.VMEM((12, 16, 128), F32),
            pltpu.VMEM((classes, tall, cols), F32),
            pltpu.VMEM((6, tall, cols), F32),
            pltpu.VMEM((tall, cols), F32),
            pltpu.VMEM((pairs + 8, 4, 128), F32),
            pltpu.VMEM((n, 12, 4, 128), F32),
            pltpu.VMEM((12, 4, 128), F32),
            pltpu.VMEM((12, 384, 512), BF16),
            pltpu.VMEM((12, NBRS, bins, 128), F32),
            pltpu.VMEM((12, bins, 128), F32),
            pltpu.VMEM((12, bins, 128), F32),
            pltpu.VMEM((2, 12, 2 * bins, 128), BF16),
            pltpu.VMEM((4, 2, 128), F32),
            pltpu.VMEM((n_lev, 4, 2, 128), F32),
            pltpu.VMEM((pairs, 2, 128), F32),
            pltpu.SemaphoreType.DMA((2, 5)),
            pltpu.SemaphoreType.DMA((2, 5)),
            pltpu.SemaphoreType.DMA((n,)),
            pltpu.SemaphoreType.DMA((n,)),
            pltpu.SemaphoreType.DMA((n_lev,)),
            pltpu.SemaphoreType.DMA((n_lev,)),
            pltpu.SemaphoreType.DMA((n,)),
            pltpu.SemaphoreType.DMA((n,)),
        ],
        compiler_params=pltpu.CompilerParams(
            collective_id=0, has_side_effects=True, vmem_limit_bytes=48 * 1024 * 1024
        ),
    )(
        ocean_conc, flow_lo, flow_hi, flow_y, open_lo, open_hi, open_y,
        settle_rate, critical_stress, erosion_rate,
        wave_energy, bands, meta, ent_cols, ent_rows, remap_weight.reshape(ent * 64, 64),
    )


def solution(mesh):
    both = ("sec", "tile")
    return jax.shard_map(
        per_device,
        mesh=mesh,
        in_specs=(
            P("lev", both, None),
            P(both, None),
            P(both, None),
            P(both, None),
            P(both, None),
            P(both, None),
            P(both, None),
            P("lev"),
            P("lev"),
            P("lev"),
            P("lev", both),
            P("lev"),
            P("lev"),
            P("lev"),
            P("lev"),
            P(None, both),
            P(None, both),
            P(both),
            P(both, None),
            P(both),
            P(both),
            P(both, None, None),
        ),
        out_specs=(P("lev", both, None), P("lev", both)),
        check_vma=False,
    )
```

```python
import functools

import jax
import jax.numpy as jnp
from jax import lax
from jax.experimental import pallas as pl
from jax.experimental.pallas import tpu as pltpu
from jax.sharding import PartitionSpec as P

OSTEPS = 4
WSTEPS = 4
NBRS = 4
KAPPA = 0.07
FORCE_SCALE = 5.0
DRAG = 50.0
TAU_CURRENT = 20.0
TAU_WAVES = 10.0
LOADS = 19
MESH = pl.DeviceIdType.MESH
F32 = jnp.float32
BF16 = jnp.bfloat16


def parts(x):
    hi = x.astype(BF16)
    lo = (x - hi.astype(F32)).astype(BF16)
    return hi, lo


def two(x, axis):
    return jnp.concatenate(parts(x), axis=axis)


def dot(a, b):
    return jnp.dot(a, b, preferred_element_type=F32)


def fold(x):
    total = x[:, 0:128]
    for i in range(1, x.shape[1] // 128):
        total = total + x[:, 128 * i : 128 * i + 128]
    return total + pltpu.roll(total, 64, axis=1)


def iota(shape, dim):
    return lax.broadcasted_iota(jnp.int32, shape, dim)


def kernel(
    sizes,
    settle, critical, erosion,
    *refs,
):
    loads = len(refs[:LOADS])
    sources, (sed_out, wave_out), local = refs[:loads], refs[loads : loads + 2], refs[loads + 2 :]
    body(sizes, settle, critical, erosion, sources, sed_out, wave_out, local[:loads], *local[loads:])


def body(
    sizes, settle, critical, erosion, sources, sed_out, wave_out, targets,
    we, meta, conc_x, fields, tau_x, table, table_in, wf,
    select, inflow, keep, energy, split, orb, orb_in, gathered,
    band_rows, ent_rows, load_sem,
    halo_send, halo_recv, table_send, table_recv, lev_send, lev_recv, orb_send, orb_recv,
):
    n_tile, n, n_lev = sizes
    (
        wave, neighbors, facing, live, flow_lo, flow_hi, flow_y, open_lo, open_hi, open_y,
        owner, slot, cell, angle, speeds, growths, orbitals, weight, conc,
    ) = targets
    copies = [
        pltpu.make_async_copy(source, target, load_sem.at[i])
        for i, (source, target) in enumerate(zip(sources, targets))
    ]
    for copy in copies:
        copy.start()
    bins = wave.shape[0]
    rows, cols = flow_lo.shape
    ent = cell.shape[0]
    pairs = 4 * n
    classes = conc.shape[0]
    sec, tile, lev = lax.axis_index("sec"), lax.axis_index("tile"), lax.axis_index("lev")
    me = sec * n_tile + tile

    def plane(peer):
        return {"sec": peer // n_tile, "tile": lax.rem(peer, n_tile)}

    barrier = pltpu.get_barrier_semaphore()

    @pl.loop(1, n)
    def _(off):
        pl.semaphore_signal(
            barrier, inc=1, device_id=plane(lax.rem(me + off, n)), device_id_type=MESH
        )

    @pl.loop(1, n_lev)
    def _(off):
        pl.semaphore_signal(
            barrier, inc=1, device_id={"lev": lax.rem(lev + off, n_lev)}, device_id_type=MESH
        )

    for copy in copies[0:4]:
        copy.wait()
    toward = facing[...]
    toward_c, toward_s = jnp.cos(toward), jnp.sin(toward)
    near_f = neighbors[...].astype(F32)
    live_f = live[...].astype(F32).reshape(1, live.shape[0])
    for j in range(4):
        lanes = slice(128 * j, 128 * j + 128)
        we[4 + j] = wave[:, lanes].astype(F32)
        meta[4 + j, 0:4, :] = near_f[:, lanes]
        meta[4 + j, 4:8, :] = toward_c[:, lanes]
        meta[4 + j, 8:12, :] = toward_s[:, lanes]
        meta[4 + j, 12:16, :] = jnp.broadcast_to(live_f[:, lanes], (4, 128))

    @pl.when(me == 0)
    def _():
        we[0:4] = jnp.zeros((4, bins, 128), F32)
        meta[0:4] = jnp.zeros((4, 16, 128), F32)
        fields[:, 0:8] = jnp.zeros((6, 8, cols), F32)
        conc_x[:, 0:8] = jnp.zeros((classes, 8, cols), F32)
        tau_x[0:8] = jnp.zeros((8, cols), F32)

    @pl.when(me == n - 1)
    def _():
        we[8:12] = jnp.zeros((4, bins, 128), F32)
        meta[8:12] = jnp.zeros((4, 16, 128), F32)
        fields[:, rows + 8 : rows + 16] = jnp.zeros((6, 8, cols), F32)
        conc_x[:, rows + 8 : rows + 16] = jnp.zeros((classes, 8, cols), F32)
        tau_x[rows + 8 : rows + 16] = jnp.zeros((8, cols), F32)

    pl.semaphore_wait(barrier, n - 1 + n_lev - 1)

    def to_right(src, dst, i):
        return pltpu.make_async_remote_copy(
            src_ref=src, dst_ref=dst,
            send_sem=halo_send.at[0, i], recv_sem=halo_recv.at[0, i],
            device_id=plane(lax.rem(me + 1, n)), device_id_type=MESH,
        )

    def to_left(src, dst, i):
        return pltpu.make_async_remote_copy(
            src_ref=src, dst_ref=dst,
            send_sem=halo_send.at[1, i], recv_sem=halo_recv.at[1, i],
            device_id=plane(lax.rem(me + n - 1, n)), device_id_type=MESH,
        )

    own, before, after = pl.ds(4, 4), pl.ds(0, 4), pl.ds(8, 4)
    top, bottom = pl.ds(8, 8), pl.ds(rows, 8)
    above, below = pl.ds(0, 8), pl.ds(rows + 8, 8)
    right = [
        to_right(meta.at[own], meta.at[before], 0),
        to_right(we.at[own], we.at[before], 1),
        to_right(fields.at[:, bottom], fields.at[:, above], 2),
        to_right(conc_x.at[:, bottom], conc_x.at[:, above], 3),
        to_right(tau_x.at[bottom], tau_x.at[above], 4),
    ]
    left = [
        to_left(meta.at[own], meta.at[after], 0),
        to_left(we.at[own], we.at[after], 1),
        to_left(fields.at[:, top], fields.at[:, below], 2),
        to_left(conc_x.at[:, top], conc_x.at[:, below], 3),
        to_left(tau_x.at[top], tau_x.at[below], 4),
    ]

    def start(items):
        @pl.when(me < n - 1)
        def _():
            for i in items:
                right[i].start()

        @pl.when(me > 0)
        def _():
            for i in items:
                left[i].start()

    def arrived(items):
        @pl.when(me > 0)
        def _():
            for i in items:
                right[i].wait_recv()

        @pl.when(me < n - 1)
        def _():
            for i in items:
                left[i].wait_recv()

    def sent(items):
        @pl.when(me < n - 1)
        def _():
            for i in items:
                right[i].wait_send()

        @pl.when(me > 0)
        def _():
            for i in items:
                left[i].wait_send()

    start([0, 1])

    for copy in copies[4:]:
        copy.wait()
    lo, hi, side = flow_lo[...].astype(F32), flow_hi[...].astype(F32), flow_y[...].astype(F32)
    ol, oh, oy = open_lo[...].astype(F32), open_hi[...].astype(F32), open_y[...].astype(F32)
    first_col = iota((rows, cols), 1) == 0

    def left_of(x):
        return jnp.where(first_col, 0.0, pltpu.roll(x, 1, axis=1))

    east = 0.5 * (lo + hi)
    north = 0.5 * (side + left_of(side))
    square = east * east + north * north
    speed = jnp.sqrt(square)
    a_y = jnp.maximum(side, 0.0) + KAPPA * oy
    b_y = jnp.minimum(side, 0.0) - KAPPA * oy
    a_hi = jnp.maximum(hi, 0.0) + KAPPA * oh
    b_hi = jnp.minimum(hi, 0.0) - KAPPA * oh
    a_lo = jnp.maximum(lo, 0.0) + KAPPA * ol
    b_lo = jnp.minimum(lo, 0.0) - KAPPA * ol
    mid = pl.ds(8, rows)
    fields[0, mid] = 1.0 - a_hi + b_lo - a_y + left_of(b_y)
    fields[1, mid] = a_lo
    fields[2, mid] = -b_hi
    fields[3, mid] = -b_y
    fields[4, mid] = left_of(a_y)
    fields[5, mid] = TAU_CURRENT * square
    for c in range(classes):
        conc_x[c, mid] = conc[c]


    per_row = cols // 64
    cells, slots = cell[...].reshape(1, ent), slot[...].reshape(1, ent)
    pair_ids = owner[...].reshape(1, ent) * 4 + slots // 2
    row_ids = cells // per_row
    ent_rows[...] = jnp.zeros(ent_rows.shape, F32)
    for i, x in enumerate([row_ids, cells % per_row, pair_ids, slots % 2]):
        ent_rows[i : i + 1, 0:ent] = x.astype(F32)
    ent_cols = ent_rows[...].T[0:ent].astype(jnp.int32)
    cell_row, cell_col = ent_cols[:, 0:1], ent_cols[:, 1:2]
    pair_col, parity = ent_cols[:, 2:3], ent_cols[:, 3:4]
    row_hot = (iota((ent, rows), 1) == cell_row).astype(F32).astype(BF16)
    forcing = jnp.concatenate(
        [
            FORCE_SCALE * east,
            FORCE_SCALE * north,
            DRAG * speed * east,
            DRAG * speed * north,
        ],
        axis=1,
    )
    picked = dot(jnp.concatenate([row_hot, row_hot], axis=1), two(forcing, 0))
    cell_mask = (iota((ent, cols), 1) // 64 == cell_col).astype(F32)
    channels = [fold(picked[:, cols * c : cols * c + cols] * cell_mask)[:, 0:64] for c in range(4)]
    group_mask = (iota((32, 512), 1) // 64 == lax.rem(iota((32, 512), 0), 8)).astype(F32)
    pieces = []
    for g in range(ent // 8):
        left_side = two(jnp.concatenate([x[8 * g : 8 * g + 8] for x in channels], axis=0), 0)
        block = lax.dot_general(
            left_side, weight[512 * g : 512 * g + 512, :],
            (((1,), (1,)), ((), ())), preferred_element_type=F32,
        )
        pieces.append(fold((block[0:32] + block[32:64]) * group_mask))
    parity_mask = (iota((ent, 128), 1) // 64 == parity).astype(F32)
    stacked = jnp.concatenate(
        [
            jnp.concatenate([x[8 * c : 8 * c + 8] for x in pieces], axis=0) * parity_mask
            for c in range(4)
        ],
        axis=1,
    )
    pair_hot = (iota((pairs, ent), 0) == pair_ids).astype(F32).astype(BF16)
    sums = dot(jnp.concatenate([pair_hot, pair_hot], axis=1), two(stacked, 0))
    table[0:4] = jnp.zeros((4, 4, 128), F32)
    table[pairs + 4 : pairs + 8] = jnp.zeros((4, 4, 128), F32)
    for c in range(4):
        table[4 : pairs + 4, c, :] = sums[:, 128 * c : 128 * c + 128]

    def table_copy(off):
        peer = lax.rem(me + off, n)
        return pltpu.make_async_remote_copy(
            src_ref=table.at[pl.ds(4 * peer, 12)], dst_ref=table_in.at[off],
            send_sem=table_send.at[off], recv_sem=table_recv.at[off],
            device_id=plane(peer), device_id_type=MESH,
        )

    @pl.loop(1, n)
    def _(off):
        table_copy(off).start()

    start([2, 3])

    arrived([0])

    @pl.loop(1, 11)
    def _(b):
        base = (4 * me - 5 + b) * 128
        near = meta[b][0:NBRS].astype(jnp.int32) - base
        for k in range(NBRS):
            hot = (iota((384, 128), 0) == near[k : k + 1, :]).astype(F32)
            select[b, :, 128 * k : 128 * k + 128] = hot.astype(BF16)

    band_rows[...] = jnp.zeros(band_rows.shape, F32)
    turn = angle[...].reshape(1, bins)
    turn_c, turn_s = jnp.cos(turn), jnp.sin(turn)
    gain_row = orbitals[...].reshape(1, bins)
    for i, x in enumerate(
        [
            turn_c, turn_s, speeds[...].reshape(1, bins), growths[...].reshape(1, bins),
            gain_row * turn_c, gain_row * turn_s,
        ]
    ):
        band_rows[i : i + 1, 0:bins] = x
    bands = band_rows[...].T[0:bins]

    wf[...] = table[pl.ds(4 * me, 12)]

    @pl.loop(1, n)
    def _(off):
        table_copy(off).wait_recv()
        wf[...] += table_in[off]

    cosine, sine = bands[:, 0:1], bands[:, 1:2]
    pace, growth = bands[:, 2:3], bands[:, 3:4]
    coef_c, coef_s = bands[:, 4:5], bands[:, 5:6]

    @pl.loop(1, 11)
    def _(b):
        w = wf[b]
        m = meta[b]
        alive = m[12:13, :]
        drift = cosine * w[0:1, :] + sine * w[1:2, :]
        rate = pace * (0.5 + 0.25 * jnp.tanh(drift)) * alive
        total = jnp.zeros((bins, 128), F32)
        for k in range(NBRS):
            flow = rate * jnp.maximum(
                -(cosine * m[4 + k : 5 + k, :] + sine * m[8 + k : 9 + k, :]), 0.0
            )
            inflow[b, k] = flow
            total = total + flow
        keep[b] = alive - total

    arrived([1])

    @pl.loop(0, 12)
    def _(b):
        w = wf[b]
        push = jnp.maximum(cosine * w[2:3, :] + sine * w[3:4, :], 0.0)
        first = (we[b] + growth * push) * meta[b][12:13, :]
        energy[b] = first
        split[0, b] = two(first, 0)

    for step in range(WSTEPS):
        now, later = step % 2, (step + 1) % 2

        @pl.loop(step + 1, 11 - step)
        def _(b):
            window = jnp.concatenate(
                [split[now, b - 1], split[now, b], split[now, b + 1]], axis=1
            )
            got = dot(window, select[b])
            new = keep[b] * energy[b]
            for k in range(NBRS):
                lanes = slice(128 * k, 128 * k + 128)
                new = new + inflow[b, k] * (got[0:bins, lanes] + got[bins : 2 * bins, lanes])
            energy[b] = new
            if step < WSTEPS - 1:
                split[later, b] = two(new, 0)

    for j in range(4):
        final = energy[4 + j]
        orb[j, 0:1, :] = jnp.sum(coef_c * final, axis=0, keepdims=True)
        orb[j, 1:2, :] = jnp.sum(coef_s * final, axis=0, keepdims=True)

    def lev_copy(off):
        return pltpu.make_async_remote_copy(
            src_ref=orb, dst_ref=orb_in.at[off],
            send_sem=lev_send.at[off], recv_sem=lev_recv.at[off],
            device_id={"lev": lax.rem(lev + off, n_lev)}, device_id_type=MESH,
        )

    for off in range(1, n_lev):
        lev_copy(off).start()
    for j in range(4):
        wave_out[:, 128 * j : 128 * j + 128] = energy[4 + j].astype(BF16)
    full = orb[...]
    for off in range(1, n_lev):
        lev_copy(off).wait_recv()
        full = full + orb_in[off]
    mine = pl.ds(4 * me, 4)
    gathered[mine] = full

    def orb_copy(off):
        return pltpu.make_async_remote_copy(
            src_ref=gathered.at[mine], dst_ref=gathered.at[mine],
            send_sem=orb_send.at[off], recv_sem=orb_recv.at[off],
            device_id=plane(lax.rem(me + off, n)), device_id_type=MESH,
        )

    def orb_arrival(off):
        source = pl.ds(4 * lax.rem(me - off + n, n), 4)
        return pltpu.make_async_remote_copy(
            src_ref=gathered.at[mine], dst_ref=gathered.at[source],
            send_sem=orb_send.at[off], recv_sem=orb_recv.at[off],
            device_id=plane(lax.rem(me + off, n)), device_id_type=MESH,
        )

    @pl.loop(1, n)
    def _(off):
        orb_copy(off).start()

    hot = (iota((ent, pairs), 1) == pair_col).astype(F32).astype(BF16)
    group_mask = (iota((ent, 512), 1) // 64 == lax.rem(iota((ent, 512), 0), 8)).astype(F32)

    @pl.loop(1, n)
    def _(off):
        orb_arrival(off).wait_recv()

    field = jnp.concatenate([gathered[:, 0, :], gathered[:, 1, :]], axis=1)
    back = dot(jnp.concatenate([hot, hot], axis=1), two(field, 0))
    wide = []
    for c in range(2):
        x = fold(back[:, 128 * c : 128 * c + 128] * parity_mask)
        wide.append(jnp.concatenate([x, x, x, x], axis=1) * group_mask)
    spread = []
    for g in range(ent // 8):
        left_side = two(jnp.concatenate([x[8 * g : 8 * g + 8] for x in wide], axis=0), 0)
        block = dot(left_side, weight[512 * g : 512 * g + 512, :])
        spread.append(block[0:16] + block[16:32])
    row_hot_t = (iota((rows, ent), 0) == row_ids).astype(F32).astype(BF16)
    placed = []
    for c in range(2):
        x = jnp.concatenate([y[8 * c : 8 * c + 8] for y in spread], axis=0)
        placed.append(jnp.concatenate([x] * (cols // 64), axis=1) * cell_mask)
    orbital = dot(
        jnp.concatenate([row_hot_t, row_hot_t], axis=1), two(jnp.concatenate(placed, axis=1), 0)
    )
    orbital_c, orbital_s = orbital[:, 0:cols], orbital[:, cols : 2 * cols]
    tau_x[mid] = TAU_WAVES * (orbital_c * orbital_c + orbital_s * orbital_s)
    start([4])
    arrived([2, 3, 4])
    stress = fields[5] + tau_x[...]
    tall = rows + 16
    for c in range(classes):
        gain = erosion[c] * jnp.maximum(stress / critical[c] - 1.0, 0.0)
        centre = fields[0] - settle[c]
        state = conc_x[c]
        for _ in range(OSTEPS):
            state = (
                centre * state
                + fields[1] * pltpu.roll(state, 1, axis=0)
                + fields[2] * pltpu.roll(state, tall - 1, axis=0)
                + fields[3] * pltpu.roll(state, cols - 1, axis=1)
                + fields[4] * pltpu.roll(state, 1, axis=1)
                + gain
            )
        sed_out[c] = state[8 : rows + 8]

    sent([0, 1, 2, 3, 4])

    @pl.loop(1, n)
    def _(off):
        table_copy(off).wait_send()
        orb_copy(off).wait_send()

    for off in range(1, n_lev):
        lev_copy(off).wait_send()


def per_device(
    ocean_conc, flow_lo, flow_hi, flow_y, open_lo, open_hi, open_y,
    settle_rate, critical_stress, erosion_rate,
    wave_energy, band_angle, band_speed, band_growth, band_orbital,
    neighbors, facing_angle, live_nodes,
    remap_owner, remap_slot, remap_cell, remap_weight,
):
    n_tile = lax.axis_size("tile")
    n = lax.axis_size("sec") * n_tile
    n_lev = lax.axis_size("lev")
    rows, cols = flow_lo.shape
    bins, nodes = wave_energy.shape
    ent = remap_cell.shape[0]
    classes = ocean_conc.shape[0]
    pairs = 4 * n
    sources = (
        wave_energy, neighbors, facing_angle, live_nodes,
        flow_lo, flow_hi, flow_y, open_lo, open_hi, open_y,
        remap_owner.reshape(ent), remap_slot, remap_cell,
        band_angle, band_speed, band_growth, band_orbital,
        remap_weight.reshape(ent * 64, 64), ocean_conc,
    )
    vmem = pl.BlockSpec(memory_space=pltpu.VMEM)
    smem = pl.BlockSpec(memory_space=pltpu.SMEM)
    tall = rows + 16
    return pl.pallas_call(
        functools.partial(kernel, (n_tile, n, n_lev)),
        out_shape=(
            jax.ShapeDtypeStruct(ocean_conc.shape, F32),
            jax.ShapeDtypeStruct(wave_energy.shape, BF16),
        ),
        in_specs=[smem] * 3 + [pl.BlockSpec(memory_space=pl.ANY)] * LOADS,
        out_specs=(vmem, vmem),
        scratch_shapes=[pltpu.VMEM(x.shape, x.dtype) for x in sources]
        + [
            pltpu.VMEM((12, bins, 128), F32),
            pltpu.VMEM((12, 16, 128), F32),
            pltpu.VMEM((classes, tall, cols), F32),
            pltpu.VMEM((6, tall, cols), F32),
            pltpu.VMEM((tall, cols), F32),
            pltpu.VMEM((pairs + 8, 4, 128), F32),
            pltpu.VMEM((n, 12, 4, 128), F32),
            pltpu.VMEM((12, 4, 128), F32),
            pltpu.VMEM((12, 384, 512), BF16),
            pltpu.VMEM((12, NBRS, bins, 128), F32),
            pltpu.VMEM((12, bins, 128), F32),
            pltpu.VMEM((12, bins, 128), F32),
            pltpu.VMEM((2, 12, 2 * bins, 128), BF16),
            pltpu.VMEM((4, 2, 128), F32),
            pltpu.VMEM((n_lev, 4, 2, 128), F32),
            pltpu.VMEM((pairs, 2, 128), F32),
            pltpu.VMEM((8, -(-bins // 128) * 128), F32),
            pltpu.VMEM((8, -(-ent // 128) * 128), F32),
            pltpu.SemaphoreType.DMA((LOADS,)),
            pltpu.SemaphoreType.DMA((2, 5)),
            pltpu.SemaphoreType.DMA((2, 5)),
            pltpu.SemaphoreType.DMA((n,)),
            pltpu.SemaphoreType.DMA((n,)),
            pltpu.SemaphoreType.DMA((n_lev,)),
            pltpu.SemaphoreType.DMA((n_lev,)),
            pltpu.SemaphoreType.DMA((n,)),
            pltpu.SemaphoreType.DMA((n,)),
        ],
        compiler_params=pltpu.CompilerParams(
            collective_id=0, has_side_effects=True, vmem_limit_bytes=56 * 1024 * 1024
        ),
    )(settle_rate, critical_stress, erosion_rate, *sources)


def solution(mesh):
    both = ("sec", "tile")
    return jax.shard_map(
        per_device,
        mesh=mesh,
        in_specs=(
            P("lev", both, None),
            P(both, None),
            P(both, None),
            P(both, None),
            P(both, None),
            P(both, None),
            P(both, None),
            P("lev"),
            P("lev"),
            P("lev"),
            P("lev", both),
            P("lev"),
            P("lev"),
            P("lev"),
            P("lev"),
            P(None, both),
            P(None, both),
            P(both),
            P(both, None),
            P(both),
            P(both),
            P(both, None, None),
        ),
        out_specs=(P("lev", both, None), P("lev", both)),
        check_vma=False,
    )
```

```python
import functools

import jax
import jax.numpy as jnp
from jax import lax
from jax.experimental import pallas as pl
from jax.experimental.pallas import tpu as pltpu
from jax.sharding import PartitionSpec as P

OSTEPS = 4
WSTEPS = 4
NBRS = 4
KAPPA = 0.07
FORCE_SCALE = 5.0
DRAG = 50.0
TAU_CURRENT = 20.0
TAU_WAVES = 10.0
LOADS = 19
MESH = pl.DeviceIdType.MESH
F32 = jnp.float32
BF16 = jnp.bfloat16


def parts(x):
    hi = x.astype(BF16)
    lo = (x - hi.astype(F32)).astype(BF16)
    return hi, lo


def two(x, axis):
    return jnp.concatenate(parts(x), axis=axis)


def dot(a, b):
    return jnp.dot(a, b, preferred_element_type=F32)


def fold(x):
    total = x[:, 0:128]
    for i in range(1, x.shape[1] // 128):
        total = total + x[:, 128 * i : 128 * i + 128]
    return total + pltpu.roll(total, 64, axis=1)


def iota(shape, dim):
    return lax.broadcasted_iota(jnp.int32, shape, dim)


def kernel(
    sizes,
    settle, critical, erosion,
    *refs,
):
    loads = len(refs[:LOADS])
    sources, (sed_out, wave_out), local = refs[:loads], refs[loads : loads + 2], refs[loads + 2 :]
    body(sizes, settle, critical, erosion, sources, sed_out, wave_out, local[:loads], *local[loads:])


def body(
    sizes, settle, critical, erosion, sources, sed_out, wave_out, targets,
    we, meta, conc_x, fields, tau_x, table, table_in, wf,
    select, inflow, keep, energy, split, orb, orb_in, gathered,
    band_rows, ent_rows, spread_bands, load_sem,
    halo_send, halo_recv, table_send, table_recv, lev_send, lev_recv, orb_send, orb_recv,
):
    n_tile, n, n_lev = sizes
    (
        wave, neighbors, facing, live, flow_lo, flow_hi, flow_y, open_lo, open_hi, open_y,
        owner, slot, cell, angle, speeds, growths, orbitals, weight, conc,
    ) = targets
    copies = [
        pltpu.make_async_copy(source, target, load_sem.at[i])
        for i, (source, target) in enumerate(zip(sources, targets))
    ]
    for copy in copies:
        copy.start()
    bins = wave.shape[0]
    rows, cols = flow_lo.shape
    ent = cell.shape[0]
    pairs = 4 * n
    classes = conc.shape[0]
    sec, tile, lev = lax.axis_index("sec"), lax.axis_index("tile"), lax.axis_index("lev")
    me = sec * n_tile + tile

    def plane(peer):
        return {"sec": peer // n_tile, "tile": lax.rem(peer, n_tile)}

    barrier = pltpu.get_barrier_semaphore()

    @pl.loop(1, n)
    def _(off):
        pl.semaphore_signal(
            barrier, inc=1, device_id=plane(lax.rem(me + off, n)), device_id_type=MESH
        )

    @pl.loop(1, n_lev)
    def _(off):
        pl.semaphore_signal(
            barrier, inc=1, device_id={"lev": lax.rem(lev + off, n_lev)}, device_id_type=MESH
        )

    for copy in copies[0:4]:
        copy.wait()
    toward = facing[...]
    toward_c, toward_s = jnp.cos(toward), jnp.sin(toward)
    near_f = neighbors[...].astype(F32)
    live_f = live[...].astype(F32).reshape(1, live.shape[0])
    for j in range(4):
        lanes = slice(128 * j, 128 * j + 128)
        we[4 + j] = wave[:, lanes].astype(F32)
        meta[4 + j, 0:4, :] = near_f[:, lanes]
        meta[4 + j, 4:8, :] = toward_c[:, lanes]
        meta[4 + j, 8:12, :] = toward_s[:, lanes]
        meta[4 + j, 12:16, :] = jnp.broadcast_to(live_f[:, lanes], (4, 128))

    @pl.when(me == 0)
    def _():
        we[0:4] = jnp.zeros((4, bins, 128), F32)
        meta[0:4] = jnp.zeros((4, 16, 128), F32)
        fields[:, 0:8] = jnp.zeros((6, 8, cols), F32)
        conc_x[:, 0:8] = jnp.zeros((classes, 8, cols), F32)
        tau_x[0:8] = jnp.zeros((8, cols), F32)

    @pl.when(me == n - 1)
    def _():
        we[8:12] = jnp.zeros((4, bins, 128), F32)
        meta[8:12] = jnp.zeros((4, 16, 128), F32)
        fields[:, rows + 8 : rows + 16] = jnp.zeros((6, 8, cols), F32)
        conc_x[:, rows + 8 : rows + 16] = jnp.zeros((classes, 8, cols), F32)
        tau_x[rows + 8 : rows + 16] = jnp.zeros((8, cols), F32)

    pl.semaphore_wait(barrier, n - 1 + n_lev - 1)

    def to_right(src, dst, i):
        return pltpu.make_async_remote_copy(
            src_ref=src, dst_ref=dst,
            send_sem=halo_send.at[0, i], recv_sem=halo_recv.at[0, i],
            device_id=plane(lax.rem(me + 1, n)), device_id_type=MESH,
        )

    def to_left(src, dst, i):
        return pltpu.make_async_remote_copy(
            src_ref=src, dst_ref=dst,
            send_sem=halo_send.at[1, i], recv_sem=halo_recv.at[1, i],
            device_id=plane(lax.rem(me + n - 1, n)), device_id_type=MESH,
        )

    own, before, after = pl.ds(4, 4), pl.ds(0, 4), pl.ds(8, 4)
    top, bottom = pl.ds(8, 8), pl.ds(rows, 8)
    above, below = pl.ds(0, 8), pl.ds(rows + 8, 8)
    right = [
        to_right(meta.at[own], meta.at[before], 0),
        to_right(we.at[own], we.at[before], 1),
        to_right(fields.at[:, bottom], fields.at[:, above], 2),
        to_right(conc_x.at[:, bottom], conc_x.at[:, above], 3),
        to_right(tau_x.at[bottom], tau_x.at[above], 4),
    ]
    left = [
        to_left(meta.at[own], meta.at[after], 0),
        to_left(we.at[own], we.at[after], 1),
        to_left(fields.at[:, top], fields.at[:, below], 2),
        to_left(conc_x.at[:, top], conc_x.at[:, below], 3),
        to_left(tau_x.at[top], tau_x.at[below], 4),
    ]

    def start(items):
        @pl.when(me < n - 1)
        def _():
            for i in items:
                right[i].start()

        @pl.when(me > 0)
        def _():
            for i in items:
                left[i].start()

    def arrived(items):
        @pl.when(me > 0)
        def _():
            for i in items:
                right[i].wait_recv()

        @pl.when(me < n - 1)
        def _():
            for i in items:
                left[i].wait_recv()

    def sent(items):
        @pl.when(me < n - 1)
        def _():
            for i in items:
                right[i].wait_send()

        @pl.when(me > 0)
        def _():
            for i in items:
                left[i].wait_send()

    start([0, 1])

    for copy in copies[4:]:
        copy.wait()
    lo, hi, side = flow_lo[...].astype(F32), flow_hi[...].astype(F32), flow_y[...].astype(F32)
    ol, oh, oy = open_lo[...].astype(F32), open_hi[...].astype(F32), open_y[...].astype(F32)
    first_col = iota((rows, cols), 1) == 0

    def left_of(x):
        return jnp.where(first_col, 0.0, pltpu.roll(x, 1, axis=1))

    mid = pl.ds(8, rows)
    east = 0.5 * (lo + hi)
    north = 0.5 * (side + left_of(side))
    square = east * east + north * north
    speed = jnp.sqrt(square)

    per_row = cols // 64
    cells, slots = cell[...].reshape(1, ent), slot[...].reshape(1, ent)
    pair_ids = owner[...].reshape(1, ent) * 4 + slots // 2
    row_ids = cells // per_row
    ent_rows[...] = jnp.zeros(ent_rows.shape, F32)
    for i, x in enumerate([row_ids, cells % per_row, pair_ids, slots % 2]):
        ent_rows[i : i + 1, 0:ent] = x.astype(F32)
    ent_cols = ent_rows[...].T[0:ent].astype(jnp.int32)
    cell_row, cell_col = ent_cols[:, 0:1], ent_cols[:, 1:2]
    pair_col, parity = ent_cols[:, 2:3], ent_cols[:, 3:4]
    row_hot = (iota((ent, rows), 1) == cell_row).astype(F32).astype(BF16)
    forcing = jnp.concatenate(
        [
            FORCE_SCALE * east,
            FORCE_SCALE * north,
            DRAG * speed * east,
            DRAG * speed * north,
        ],
        axis=1,
    )
    picked = dot(jnp.concatenate([row_hot, row_hot], axis=1), two(forcing, 0))
    cell_mask = (iota((ent, cols), 1) // 64 == cell_col).astype(F32)
    channels = [fold(picked[:, cols * c : cols * c + cols] * cell_mask)[:, 0:64] for c in range(4)]
    group_mask = (iota((32, 512), 1) // 64 == lax.rem(iota((32, 512), 0), 8)).astype(F32)
    pieces = []
    for g in range(ent // 8):
        left_side = two(jnp.concatenate([x[8 * g : 8 * g + 8] for x in channels], axis=0), 0)
        block = lax.dot_general(
            left_side, weight[512 * g : 512 * g + 512, :],
            (((1,), (1,)), ((), ())), preferred_element_type=F32,
        )
        pieces.append(fold((block[0:32] + block[32:64]) * group_mask))
    parity_mask = (iota((ent, 128), 1) // 64 == parity).astype(F32)
    stacked = jnp.concatenate(
        [
            jnp.concatenate([x[8 * c : 8 * c + 8] for x in pieces], axis=0) * parity_mask
            for c in range(4)
        ],
        axis=1,
    )
    pair_hot = (iota((pairs, ent), 0) == pair_ids).astype(F32).astype(BF16)
    sums = dot(jnp.concatenate([pair_hot, pair_hot], axis=1), two(stacked, 0))
    table[0:4] = jnp.zeros((4, 4, 128), F32)
    table[pairs + 4 : pairs + 8] = jnp.zeros((4, 4, 128), F32)
    for c in range(4):
        table[4 : pairs + 4, c, :] = sums[:, 128 * c : 128 * c + 128]

    def table_copy(off):
        peer = lax.rem(me + off, n)
        return pltpu.make_async_remote_copy(
            src_ref=table.at[pl.ds(4 * peer, 12)], dst_ref=table_in.at[off],
            send_sem=table_send.at[off], recv_sem=table_recv.at[off],
            device_id=plane(peer), device_id_type=MESH,
        )

    @pl.loop(1, n)
    def _(off):
        table_copy(off).start()


    a_y = jnp.maximum(side, 0.0) + KAPPA * oy
    b_y = jnp.minimum(side, 0.0) - KAPPA * oy
    a_hi = jnp.maximum(hi, 0.0) + KAPPA * oh
    b_hi = jnp.minimum(hi, 0.0) - KAPPA * oh
    a_lo = jnp.maximum(lo, 0.0) + KAPPA * ol
    b_lo = jnp.minimum(lo, 0.0) - KAPPA * ol
    fields[0, mid] = 1.0 - a_hi + b_lo - a_y + left_of(b_y)
    fields[1, mid] = a_lo
    fields[2, mid] = -b_hi
    fields[3, mid] = -b_y
    fields[4, mid] = left_of(a_y)
    fields[5, mid] = TAU_CURRENT * square
    for c in range(classes):
        conc_x[c, mid] = conc[c]
    start([2, 3])

    arrived([0])

    @pl.loop(1, 11)
    def _(b):
        base = (4 * me - 5 + b) * 128
        near = meta[b][0:NBRS].astype(jnp.int32) - base
        for k in range(NBRS):
            hot = (iota((384, 128), 0) == near[k : k + 1, :]).astype(F32)
            select[b, :, 128 * k : 128 * k + 128] = hot.astype(BF16)

    band_rows[...] = jnp.zeros(band_rows.shape, F32)
    turn = angle[...].reshape(1, bins)
    turn_c, turn_s = jnp.cos(turn), jnp.sin(turn)
    gain_row = orbitals[...].reshape(1, bins)
    for i, x in enumerate(
        [
            turn_c, turn_s, speeds[...].reshape(1, bins), growths[...].reshape(1, bins),
            gain_row * turn_c, gain_row * turn_s,
        ]
    ):
        band_rows[i : i + 1, 0:bins] = x
    bands = band_rows[...].T[0:bins]
    for i in range(6):
        spread_bands[i] = jnp.broadcast_to(bands[:, i : i + 1], (bins, 128))

    wf[...] = table[pl.ds(4 * me, 12)]

    @pl.loop(1, n)
    def _(off):
        table_copy(off).wait_recv()
        wf[...] += table_in[off]

    @pl.loop(1, 11, unroll=2)
    def _(b):
        cosine, sine, pace = spread_bands[0], spread_bands[1], spread_bands[2]
        w = wf[b]
        m = meta[b]
        alive = m[12:13, :]
        drift = cosine * w[0:1, :] + sine * w[1:2, :]
        rate = pace * (0.5 + 0.25 * jnp.tanh(drift)) * alive
        total = jnp.zeros((bins, 128), F32)
        for k in range(NBRS):
            flow = rate * jnp.maximum(
                -(cosine * m[4 + k : 5 + k, :] + sine * m[8 + k : 9 + k, :]), 0.0
            )
            inflow[b, k] = flow
            total = total + flow
        keep[b] = alive - total

    arrived([1])

    @pl.loop(0, 12, unroll=2)
    def _(b):
        cosine, sine, growth = spread_bands[0], spread_bands[1], spread_bands[3]
        w = wf[b]
        push = jnp.maximum(cosine * w[2:3, :] + sine * w[3:4, :], 0.0)
        first = (we[b] + growth * push) * meta[b][12:13, :]
        energy[b] = first
        split[0, b] = two(first, 0)

    for step in range(WSTEPS):
        now, later = step % 2, (step + 1) % 2

        @pl.loop(step + 1, 11 - step, unroll=2)
        def _(b):
            window = jnp.concatenate(
                [split[now, b - 1], split[now, b], split[now, b + 1]], axis=1
            )
            got = dot(window, select[b])
            new = keep[b] * energy[b]
            for k in range(NBRS):
                lanes = slice(128 * k, 128 * k + 128)
                new = new + inflow[b, k] * (got[0:bins, lanes] + got[bins : 2 * bins, lanes])
            energy[b] = new
            if step < WSTEPS - 1:
                split[later, b] = two(new, 0)

    for j in range(4):
        final = energy[4 + j]
        orb[j, 0:1, :] = jnp.sum(spread_bands[4] * final, axis=0, keepdims=True)
        orb[j, 1:2, :] = jnp.sum(spread_bands[5] * final, axis=0, keepdims=True)

    def lev_copy(off):
        return pltpu.make_async_remote_copy(
            src_ref=orb, dst_ref=orb_in.at[off],
            send_sem=lev_send.at[off], recv_sem=lev_recv.at[off],
            device_id={"lev": lax.rem(lev + off, n_lev)}, device_id_type=MESH,
        )

    for off in range(1, n_lev):
        lev_copy(off).start()
    for j in range(4):
        wave_out[:, 128 * j : 128 * j + 128] = energy[4 + j].astype(BF16)
    full = orb[...]
    for off in range(1, n_lev):
        lev_copy(off).wait_recv()
        full = full + orb_in[off]
    mine = pl.ds(4 * me, 4)
    gathered[mine] = full

    def orb_copy(off):
        return pltpu.make_async_remote_copy(
            src_ref=gathered.at[mine], dst_ref=gathered.at[mine],
            send_sem=orb_send.at[off], recv_sem=orb_recv.at[off],
            device_id=plane(lax.rem(me + off, n)), device_id_type=MESH,
        )

    def orb_arrival(off):
        source = pl.ds(4 * lax.rem(me - off + n, n), 4)
        return pltpu.make_async_remote_copy(
            src_ref=gathered.at[mine], dst_ref=gathered.at[source],
            send_sem=orb_send.at[off], recv_sem=orb_recv.at[off],
            device_id=plane(lax.rem(me + off, n)), device_id_type=MESH,
        )

    @pl.loop(1, n)
    def _(off):
        orb_copy(off).start()

    hot = (iota((ent, pairs), 1) == pair_col).astype(F32).astype(BF16)
    group_mask = (iota((ent, 512), 1) // 64 == lax.rem(iota((ent, 512), 0), 8)).astype(F32)

    @pl.loop(1, n)
    def _(off):
        orb_arrival(off).wait_recv()

    field = jnp.concatenate([gathered[:, 0, :], gathered[:, 1, :]], axis=1)
    back = dot(jnp.concatenate([hot, hot], axis=1), two(field, 0))
    wide = []
    for c in range(2):
        x = fold(back[:, 128 * c : 128 * c + 128] * parity_mask)
        wide.append(jnp.concatenate([x, x, x, x], axis=1) * group_mask)
    spread = []
    for g in range(ent // 8):
        left_side = two(jnp.concatenate([x[8 * g : 8 * g + 8] for x in wide], axis=0), 0)
        block = dot(left_side, weight[512 * g : 512 * g + 512, :])
        spread.append(block[0:16] + block[16:32])
    row_hot_t = (iota((rows, ent), 0) == row_ids).astype(F32).astype(BF16)
    placed = []
    for c in range(2):
        x = jnp.concatenate([y[8 * c : 8 * c + 8] for y in spread], axis=0)
        placed.append(jnp.concatenate([x] * (cols // 64), axis=1) * cell_mask)
    orbital = dot(
        jnp.concatenate([row_hot_t, row_hot_t], axis=1), two(jnp.concatenate(placed, axis=1), 0)
    )
    orbital_c, orbital_s = orbital[:, 0:cols], orbital[:, cols : 2 * cols]
    tau_x[mid] = TAU_WAVES * (orbital_c * orbital_c + orbital_s * orbital_s)
    start([4])
    arrived([2, 3, 4])
    stress = fields[5] + tau_x[...]
    tall = rows + 16
    for c in range(classes):
        gain = erosion[c] * jnp.maximum(stress / critical[c] - 1.0, 0.0)
        centre = fields[0] - settle[c]
        state = conc_x[c]
        for _ in range(OSTEPS):
            state = (
                centre * state
                + fields[1] * pltpu.roll(state, 1, axis=0)
                + fields[2] * pltpu.roll(state, tall - 1, axis=0)
                + fields[3] * pltpu.roll(state, cols - 1, axis=1)
                + fields[4] * pltpu.roll(state, 1, axis=1)
                + gain
            )
        sed_out[c] = state[8 : rows + 8]

    sent([0, 1, 2, 3, 4])

    @pl.loop(1, n)
    def _(off):
        table_copy(off).wait_send()
        orb_copy(off).wait_send()

    for off in range(1, n_lev):
        lev_copy(off).wait_send()


def per_device(
    ocean_conc, flow_lo, flow_hi, flow_y, open_lo, open_hi, open_y,
    settle_rate, critical_stress, erosion_rate,
    wave_energy, band_angle, band_speed, band_growth, band_orbital,
    neighbors, facing_angle, live_nodes,
    remap_owner, remap_slot, remap_cell, remap_weight,
):
    n_tile = lax.axis_size("tile")
    n = lax.axis_size("sec") * n_tile
    n_lev = lax.axis_size("lev")
    rows, cols = flow_lo.shape
    bins, nodes = wave_energy.shape
    ent = remap_cell.shape[0]
    classes = ocean_conc.shape[0]
    pairs = 4 * n
    sources = (
        wave_energy, neighbors, facing_angle, live_nodes,
        flow_lo, flow_hi, flow_y, open_lo, open_hi, open_y,
        remap_owner.reshape(ent), remap_slot, remap_cell,
        band_angle, band_speed, band_growth, band_orbital,
        remap_weight.reshape(ent * 64, 64), ocean_conc,
    )
    vmem = pl.BlockSpec(memory_space=pltpu.VMEM)
    smem = pl.BlockSpec(memory_space=pltpu.SMEM)
    tall = rows + 16
    return pl.pallas_call(
        functools.partial(kernel, (n_tile, n, n_lev)),
        out_shape=(
            jax.ShapeDtypeStruct(ocean_conc.shape, F32),
            jax.ShapeDtypeStruct(wave_energy.shape, BF16),
        ),
        in_specs=[smem] * 3 + [pl.BlockSpec(memory_space=pl.ANY)] * LOADS,
        out_specs=(vmem, vmem),
        scratch_shapes=[pltpu.VMEM(x.shape, x.dtype) for x in sources]
        + [
            pltpu.VMEM((12, bins, 128), F32),
            pltpu.VMEM((12, 16, 128), F32),
            pltpu.VMEM((classes, tall, cols), F32),
            pltpu.VMEM((6, tall, cols), F32),
            pltpu.VMEM((tall, cols), F32),
            pltpu.VMEM((pairs + 8, 4, 128), F32),
            pltpu.VMEM((n, 12, 4, 128), F32),
            pltpu.VMEM((12, 4, 128), F32),
            pltpu.VMEM((12, 384, 512), BF16),
            pltpu.VMEM((12, NBRS, bins, 128), F32),
            pltpu.VMEM((12, bins, 128), F32),
            pltpu.VMEM((12, bins, 128), F32),
            pltpu.VMEM((2, 12, 2 * bins, 128), BF16),
            pltpu.VMEM((4, 2, 128), F32),
            pltpu.VMEM((n_lev, 4, 2, 128), F32),
            pltpu.VMEM((pairs, 2, 128), F32),
            pltpu.VMEM((8, -(-bins // 128) * 128), F32),
            pltpu.VMEM((8, -(-ent // 128) * 128), F32),
            pltpu.VMEM((6, bins, 128), F32),
            pltpu.SemaphoreType.DMA((LOADS,)),
            pltpu.SemaphoreType.DMA((2, 5)),
            pltpu.SemaphoreType.DMA((2, 5)),
            pltpu.SemaphoreType.DMA((n,)),
            pltpu.SemaphoreType.DMA((n,)),
            pltpu.SemaphoreType.DMA((n_lev,)),
            pltpu.SemaphoreType.DMA((n_lev,)),
            pltpu.SemaphoreType.DMA((n,)),
            pltpu.SemaphoreType.DMA((n,)),
        ],
        compiler_params=pltpu.CompilerParams(
            collective_id=0, has_side_effects=True, vmem_limit_bytes=56 * 1024 * 1024
        ),
    )(settle_rate, critical_stress, erosion_rate, *sources)


def solution(mesh):
    both = ("sec", "tile")
    return jax.shard_map(
        per_device,
        mesh=mesh,
        in_specs=(
            P("lev", both, None),
            P(both, None),
            P(both, None),
            P(both, None),
            P(both, None),
            P(both, None),
            P(both, None),
            P("lev"),
            P("lev"),
            P("lev"),
            P("lev", both),
            P("lev"),
            P("lev"),
            P("lev"),
            P("lev"),
            P(None, both),
            P(None, both),
            P(both),
            P(both, None),
            P(both),
            P(both),
            P(both, None, None),
        ),
        out_specs=(P("lev", both, None), P("lev", both)),
        check_vma=False,
    )
```

```python
import functools

import jax
import jax.numpy as jnp
from jax import lax
from jax.experimental import pallas as pl
from jax.experimental.pallas import tpu as pltpu
from jax.sharding import PartitionSpec as P

OSTEPS = 4
WSTEPS = 4
NBRS = 4
KAPPA = 0.07
FORCE_SCALE = 5.0
DRAG = 50.0
TAU_CURRENT = 20.0
TAU_WAVES = 10.0
LOADS = 19
MESH = pl.DeviceIdType.MESH
F32 = jnp.float32
BF16 = jnp.bfloat16


def parts(x):
    hi = x.astype(BF16)
    lo = (x - hi.astype(F32)).astype(BF16)
    return hi, lo


def two(x, axis):
    return jnp.concatenate(parts(x), axis=axis)


def dot(a, b):
    return jnp.dot(a, b, preferred_element_type=F32)


def fold(x):
    total = x[:, 0:128]
    for i in range(1, x.shape[1] // 128):
        total = total + x[:, 128 * i : 128 * i + 128]
    return total + pltpu.roll(total, 64, axis=1)


def iota(shape, dim):
    return lax.broadcasted_iota(jnp.int32, shape, dim)


def kernel(
    sizes,
    settle, critical, erosion,
    *refs,
):
    loads = len(refs[:LOADS])
    sources, (sed_out, wave_out), local = refs[:loads], refs[loads : loads + 2], refs[loads + 2 :]
    body(sizes, settle, critical, erosion, sources, sed_out, wave_out, local[:loads], *local[loads:])


def body(
    sizes, settle, critical, erosion, sources, sed_out, wave_out, targets,
    we, meta, conc_x, fields, tau_x, table, table_in, wf,
    select, inflow, keep, energy, split, orb, orb_in, gathered,
    band_rows, ent_rows, spread_bands, load_sem,
    halo_send, halo_recv, table_send, table_recv, lev_send, lev_recv, orb_send, orb_recv,
):
    n_tile, n, n_lev = sizes
    (
        wave, neighbors, facing, live, flow_lo, flow_hi, flow_y, open_lo, open_hi, open_y,
        owner, slot, cell, angle, speeds, growths, orbitals, weight, conc,
    ) = targets
    copies = [
        pltpu.make_async_copy(source, target, load_sem.at[i])
        for i, (source, target) in enumerate(zip(sources, targets))
    ]
    for copy in copies:
        copy.start()
    bins = wave.shape[0]
    rows, cols = flow_lo.shape
    ent = cell.shape[0]
    pairs = 4 * n
    classes = conc.shape[0]
    sec, tile, lev = lax.axis_index("sec"), lax.axis_index("tile"), lax.axis_index("lev")
    me = sec * n_tile + tile

    def plane(peer):
        return {"sec": peer // n_tile, "tile": lax.rem(peer, n_tile)}

    barrier = pltpu.get_barrier_semaphore()

    @pl.loop(1, n)
    def _(off):
        pl.semaphore_signal(
            barrier, inc=1, device_id=plane(lax.rem(me + off, n)), device_id_type=MESH
        )

    @pl.loop(1, n_lev)
    def _(off):
        pl.semaphore_signal(
            barrier, inc=1, device_id={"lev": lax.rem(lev + off, n_lev)}, device_id_type=MESH
        )

    for copy in copies[0:4]:
        copy.wait()
    toward = facing[...]
    toward_c, toward_s = jnp.cos(toward), jnp.sin(toward)
    near_f = neighbors[...].astype(F32)
    live_f = live[...].astype(F32).reshape(1, live.shape[0])
    for j in range(4):
        lanes = slice(128 * j, 128 * j + 128)
        we[4 + j] = wave[:, lanes].astype(F32)
        meta[4 + j, 0:4, :] = near_f[:, lanes]
        meta[4 + j, 4:8, :] = toward_c[:, lanes]
        meta[4 + j, 8:12, :] = toward_s[:, lanes]
        meta[4 + j, 12:16, :] = jnp.broadcast_to(live_f[:, lanes], (4, 128))

    @pl.when(me == 0)
    def _():
        we[0:4] = jnp.zeros((4, bins, 128), F32)
        meta[0:4] = jnp.zeros((4, 16, 128), F32)
        fields[:, 0:8] = jnp.zeros((6, 8, cols), F32)
        conc_x[:, 0:8] = jnp.zeros((classes, 8, cols), F32)
        tau_x[0:8] = jnp.zeros((8, cols), F32)

    @pl.when(me == n - 1)
    def _():
        we[8:12] = jnp.zeros((4, bins, 128), F32)
        meta[8:12] = jnp.zeros((4, 16, 128), F32)
        fields[:, rows + 8 : rows + 16] = jnp.zeros((6, 8, cols), F32)
        conc_x[:, rows + 8 : rows + 16] = jnp.zeros((classes, 8, cols), F32)
        tau_x[rows + 8 : rows + 16] = jnp.zeros((8, cols), F32)

    pl.semaphore_wait(barrier, n - 1 + n_lev - 1)

    def to_right(src, dst, i):
        return pltpu.make_async_remote_copy(
            src_ref=src, dst_ref=dst,
            send_sem=halo_send.at[0, i], recv_sem=halo_recv.at[0, i],
            device_id=plane(lax.rem(me + 1, n)), device_id_type=MESH,
        )

    def to_left(src, dst, i):
        return pltpu.make_async_remote_copy(
            src_ref=src, dst_ref=dst,
            send_sem=halo_send.at[1, i], recv_sem=halo_recv.at[1, i],
            device_id=plane(lax.rem(me + n - 1, n)), device_id_type=MESH,
        )

    own, before, after = pl.ds(4, 4), pl.ds(0, 4), pl.ds(8, 4)
    top, bottom = pl.ds(8, 8), pl.ds(rows, 8)
    above, below = pl.ds(0, 8), pl.ds(rows + 8, 8)
    right = [
        to_right(meta.at[own], meta.at[before], 0),
        to_right(we.at[own], we.at[before], 1),
        to_right(fields.at[:, bottom], fields.at[:, above], 2),
        to_right(conc_x.at[:, bottom], conc_x.at[:, above], 3),
        to_right(tau_x.at[bottom], tau_x.at[above], 4),
    ]
    left = [
        to_left(meta.at[own], meta.at[after], 0),
        to_left(we.at[own], we.at[after], 1),
        to_left(fields.at[:, top], fields.at[:, below], 2),
        to_left(conc_x.at[:, top], conc_x.at[:, below], 3),
        to_left(tau_x.at[top], tau_x.at[below], 4),
    ]

    def start(items):
        @pl.when(me < n - 1)
        def _():
            for i in items:
                right[i].start()

        @pl.when(me > 0)
        def _():
            for i in items:
                left[i].start()

    def arrived(items):
        @pl.when(me > 0)
        def _():
            for i in items:
                right[i].wait_recv()

        @pl.when(me < n - 1)
        def _():
            for i in items:
                left[i].wait_recv()

    def sent(items):
        @pl.when(me < n - 1)
        def _():
            for i in items:
                right[i].wait_send()

        @pl.when(me > 0)
        def _():
            for i in items:
                left[i].wait_send()

    start([0, 1])

    for copy in copies[4:]:
        copy.wait()
    lo, hi, side = flow_lo[...].astype(F32), flow_hi[...].astype(F32), flow_y[...].astype(F32)
    ol, oh, oy = open_lo[...].astype(F32), open_hi[...].astype(F32), open_y[...].astype(F32)
    first_col = iota((rows, cols), 1) == 0

    def left_of(x):
        return jnp.where(first_col, 0.0, pltpu.roll(x, 1, axis=1))

    mid = pl.ds(8, rows)
    east = 0.5 * (lo + hi)
    north = 0.5 * (side + left_of(side))
    square = east * east + north * north
    speed = jnp.sqrt(square)

    per_row = cols // 64
    cells, slots = cell[...].reshape(1, ent), slot[...].reshape(1, ent)
    pair_ids = owner[...].reshape(1, ent) * 4 + slots // 2
    row_ids = cells // per_row
    ent_rows[...] = jnp.zeros(ent_rows.shape, F32)
    for i, x in enumerate([row_ids, cells % per_row, pair_ids, slots % 2]):
        ent_rows[i : i + 1, 0:ent] = x.astype(F32)
    ent_cols = ent_rows[...].T[0:ent].astype(jnp.int32)
    cell_row, cell_col = ent_cols[:, 0:1], ent_cols[:, 1:2]
    pair_col, parity = ent_cols[:, 2:3], ent_cols[:, 3:4]
    row_hot = (iota((ent, rows), 1) == cell_row).astype(F32).astype(BF16)
    forcing = jnp.concatenate(
        [
            FORCE_SCALE * east,
            FORCE_SCALE * north,
            DRAG * speed * east,
            DRAG * speed * north,
        ],
        axis=1,
    )
    picked = dot(jnp.concatenate([row_hot, row_hot], axis=1), two(forcing, 0))
    cell_mask = (iota((ent, cols), 1) // 64 == cell_col).astype(F32)
    channels = [fold(picked[:, cols * c : cols * c + cols] * cell_mask)[:, 0:64] for c in range(4)]
    group_mask = (iota((32, 512), 1) // 64 == lax.rem(iota((32, 512), 0), 8)).astype(F32)
    pieces = []
    for g in range(ent // 8):
        left_side = two(jnp.concatenate([x[8 * g : 8 * g + 8] for x in channels], axis=0), 0)
        block = lax.dot_general(
            left_side, weight[512 * g : 512 * g + 512, :],
            (((1,), (1,)), ((), ())), preferred_element_type=F32,
        )
        pieces.append(fold((block[0:32] + block[32:64]) * group_mask))
    parity_mask = (iota((ent, 128), 1) // 64 == parity).astype(F32)
    stacked = jnp.concatenate(
        [
            jnp.concatenate([x[8 * c : 8 * c + 8] for x in pieces], axis=0) * parity_mask
            for c in range(4)
        ],
        axis=1,
    )
    pair_hot = (iota((pairs, ent), 0) == pair_ids).astype(F32).astype(BF16)
    sums = dot(jnp.concatenate([pair_hot, pair_hot], axis=1), two(stacked, 0))
    table[0:4] = jnp.zeros((4, 4, 128), F32)
    table[pairs + 4 : pairs + 8] = jnp.zeros((4, 4, 128), F32)
    for c in range(4):
        table[4 : pairs + 4, c, :] = sums[:, 128 * c : 128 * c + 128]

    def table_copy(off):
        peer = lax.rem(me + off, n)
        return pltpu.make_async_remote_copy(
            src_ref=table.at[pl.ds(4 * peer, 12)], dst_ref=table_in.at[off],
            send_sem=table_send.at[off], recv_sem=table_recv.at[off],
            device_id=plane(peer), device_id_type=MESH,
        )

    @pl.loop(1, n)
    def _(off):
        table_copy(off).start()


    a_y = jnp.maximum(side, 0.0) + KAPPA * oy
    b_y = jnp.minimum(side, 0.0) - KAPPA * oy
    a_hi = jnp.maximum(hi, 0.0) + KAPPA * oh
    b_hi = jnp.minimum(hi, 0.0) - KAPPA * oh
    a_lo = jnp.maximum(lo, 0.0) + KAPPA * ol
    b_lo = jnp.minimum(lo, 0.0) - KAPPA * ol
    fields[0, mid] = 1.0 - a_hi + b_lo - a_y + left_of(b_y)
    fields[1, mid] = a_lo
    fields[2, mid] = -b_hi
    fields[3, mid] = -b_y
    fields[4, mid] = left_of(a_y)
    fields[5, mid] = TAU_CURRENT * square
    for c in range(classes):
        conc_x[c, mid] = conc[c]
    start([2, 3])

    arrived([0])

    @pl.loop(1, 11, unroll=2)
    def _(b):
        base = (4 * me - 5 + b) * 128
        near = meta[b][0:NBRS].astype(jnp.int32) - base
        for k in range(NBRS):
            hot = (iota((384, 128), 0) == near[k : k + 1, :]).astype(F32)
            select[b, :, 128 * k : 128 * k + 128] = hot.astype(BF16)

    band_rows[...] = jnp.zeros(band_rows.shape, F32)
    turn = angle[...].reshape(1, bins)
    turn_c, turn_s = jnp.cos(turn), jnp.sin(turn)
    gain_row = orbitals[...].reshape(1, bins)
    for i, x in enumerate(
        [
            turn_c, turn_s, speeds[...].reshape(1, bins), growths[...].reshape(1, bins),
            gain_row * turn_c, gain_row * turn_s,
        ]
    ):
        band_rows[i : i + 1, 0:bins] = x
    bands = band_rows[...].T[0:bins]
    for i in range(6):
        spread_bands[i] = jnp.broadcast_to(bands[:, i : i + 1], (bins, 128))

    wf[...] = table[pl.ds(4 * me, 12)]

    @pl.loop(1, n)
    def _(off):
        table_copy(off).wait_recv()
        wf[...] += table_in[off]

    @pl.loop(1, 11, unroll=2)
    def _(b):
        cosine, sine, pace = spread_bands[0], spread_bands[1], spread_bands[2]
        w = wf[b]
        m = meta[b]
        alive = m[12:13, :]
        drift = cosine * w[0:1, :] + sine * w[1:2, :]
        rate = pace * (0.5 + 0.25 * jnp.tanh(drift)) * alive
        total = jnp.zeros((bins, 128), F32)
        for k in range(NBRS):
            flow = rate * jnp.maximum(
                -(cosine * m[4 + k : 5 + k, :] + sine * m[8 + k : 9 + k, :]), 0.0
            )
            inflow[b, k] = flow
            total = total + flow
        keep[b] = alive - total

    arrived([1])

    @pl.loop(0, 12, unroll=2)
    def _(b):
        cosine, sine, growth = spread_bands[0], spread_bands[1], spread_bands[3]
        w = wf[b]
        push = jnp.maximum(cosine * w[2:3, :] + sine * w[3:4, :], 0.0)
        first = (we[b] + growth * push) * meta[b][12:13, :]
        energy[b] = first
        split[0, b] = two(first, 0)

    for step in range(WSTEPS):
        now, later = step % 2, (step + 1) % 2

        @pl.loop(step + 1, 11 - step, unroll=5 - step)
        def _(b):
            window = jnp.concatenate(
                [split[now, b - 1], split[now, b], split[now, b + 1]], axis=1
            )
            got = dot(window, select[b])
            new = keep[b] * energy[b]
            for k in range(NBRS):
                lanes = slice(128 * k, 128 * k + 128)
                new = new + inflow[b, k] * (got[0:bins, lanes] + got[bins : 2 * bins, lanes])
            energy[b] = new
            if step < WSTEPS - 1:
                split[later, b] = two(new, 0)

    for j in range(4):
        final = energy[4 + j]
        orb[j, 0:1, :] = jnp.sum(spread_bands[4] * final, axis=0, keepdims=True)
        orb[j, 1:2, :] = jnp.sum(spread_bands[5] * final, axis=0, keepdims=True)

    def lev_copy(off):
        return pltpu.make_async_remote_copy(
            src_ref=orb, dst_ref=orb_in.at[off],
            send_sem=lev_send.at[off], recv_sem=lev_recv.at[off],
            device_id={"lev": lax.rem(lev + off, n_lev)}, device_id_type=MESH,
        )

    for off in range(1, n_lev):
        lev_copy(off).start()
    for j in range(4):
        wave_out[:, 128 * j : 128 * j + 128] = energy[4 + j].astype(BF16)
    full = orb[...]
    for off in range(1, n_lev):
        lev_copy(off).wait_recv()
        full = full + orb_in[off]
    mine = pl.ds(4 * me, 4)
    gathered[mine] = full

    def orb_copy(off):
        return pltpu.make_async_remote_copy(
            src_ref=gathered.at[mine], dst_ref=gathered.at[mine],
            send_sem=orb_send.at[off], recv_sem=orb_recv.at[off],
            device_id=plane(lax.rem(me + off, n)), device_id_type=MESH,
        )

    def orb_arrival(off):
        source = pl.ds(4 * lax.rem(me - off + n, n), 4)
        return pltpu.make_async_remote_copy(
            src_ref=gathered.at[mine], dst_ref=gathered.at[source],
            send_sem=orb_send.at[off], recv_sem=orb_recv.at[off],
            device_id=plane(lax.rem(me + off, n)), device_id_type=MESH,
        )

    @pl.loop(1, n)
    def _(off):
        orb_copy(off).start()

    hot = (iota((ent, pairs), 1) == pair_col).astype(F32).astype(BF16)
    group_mask = (iota((ent, 512), 1) // 64 == lax.rem(iota((ent, 512), 0), 8)).astype(F32)

    @pl.loop(1, n)
    def _(off):
        orb_arrival(off).wait_recv()

    field = jnp.concatenate([gathered[:, 0, :], gathered[:, 1, :]], axis=1)
    back = dot(jnp.concatenate([hot, hot], axis=1), two(field, 0))
    wide = []
    for c in range(2):
        x = fold(back[:, 128 * c : 128 * c + 128] * parity_mask)
        wide.append(jnp.concatenate([x, x, x, x], axis=1) * group_mask)
    spread = []
    for g in range(ent // 8):
        left_side = two(jnp.concatenate([x[8 * g : 8 * g + 8] for x in wide], axis=0), 0)
        block = dot(left_side, weight[512 * g : 512 * g + 512, :])
        spread.append(block[0:16] + block[16:32])
    row_hot_t = (iota((rows, ent), 0) == row_ids).astype(F32).astype(BF16)
    placed = []
    for c in range(2):
        x = jnp.concatenate([y[8 * c : 8 * c + 8] for y in spread], axis=0)
        placed.append(jnp.concatenate([x] * (cols // 64), axis=1) * cell_mask)
    orbital = dot(
        jnp.concatenate([row_hot_t, row_hot_t], axis=1), two(jnp.concatenate(placed, axis=1), 0)
    )
    orbital_c, orbital_s = orbital[:, 0:cols], orbital[:, cols : 2 * cols]
    tau_x[mid] = TAU_WAVES * (orbital_c * orbital_c + orbital_s * orbital_s)
    start([4])
    arrived([2, 3, 4])
    stress = fields[5] + tau_x[...]
    tall = rows + 16
    for c in range(classes):
        gain = erosion[c] * jnp.maximum(stress / critical[c] - 1.0, 0.0)
        centre = fields[0] - settle[c]
        state = conc_x[c]
        for _ in range(OSTEPS):
            state = (
                centre * state
                + fields[1] * pltpu.roll(state, 1, axis=0)
                + fields[2] * pltpu.roll(state, tall - 1, axis=0)
                + fields[3] * pltpu.roll(state, cols - 1, axis=1)
                + fields[4] * pltpu.roll(state, 1, axis=1)
                + gain
            )
        sed_out[c] = state[8 : rows + 8]

    sent([0, 1, 2, 3, 4])

    @pl.loop(1, n)
    def _(off):
        table_copy(off).wait_send()
        orb_copy(off).wait_send()

    for off in range(1, n_lev):
        lev_copy(off).wait_send()


def per_device(
    ocean_conc, flow_lo, flow_hi, flow_y, open_lo, open_hi, open_y,
    settle_rate, critical_stress, erosion_rate,
    wave_energy, band_angle, band_speed, band_growth, band_orbital,
    neighbors, facing_angle, live_nodes,
    remap_owner, remap_slot, remap_cell, remap_weight,
):
    n_tile = lax.axis_size("tile")
    n = lax.axis_size("sec") * n_tile
    n_lev = lax.axis_size("lev")
    rows, cols = flow_lo.shape
    bins, nodes = wave_energy.shape
    ent = remap_cell.shape[0]
    classes = ocean_conc.shape[0]
    pairs = 4 * n
    sources = (
        wave_energy, neighbors, facing_angle, live_nodes,
        flow_lo, flow_hi, flow_y, open_lo, open_hi, open_y,
        remap_owner.reshape(ent), remap_slot, remap_cell,
        band_angle, band_speed, band_growth, band_orbital,
        remap_weight.reshape(ent * 64, 64), ocean_conc,
    )
    vmem = pl.BlockSpec(memory_space=pltpu.VMEM)
    smem = pl.BlockSpec(memory_space=pltpu.SMEM)
    tall = rows + 16
    return pl.pallas_call(
        functools.partial(kernel, (n_tile, n, n_lev)),
        out_shape=(
            jax.ShapeDtypeStruct(ocean_conc.shape, F32),
            jax.ShapeDtypeStruct(wave_energy.shape, BF16),
        ),
        in_specs=[smem] * 3 + [pl.BlockSpec(memory_space=pl.ANY)] * LOADS,
        out_specs=(vmem, vmem),
        scratch_shapes=[pltpu.VMEM(x.shape, x.dtype) for x in sources]
        + [
            pltpu.VMEM((12, bins, 128), F32),
            pltpu.VMEM((12, 16, 128), F32),
            pltpu.VMEM((classes, tall, cols), F32),
            pltpu.VMEM((6, tall, cols), F32),
            pltpu.VMEM((tall, cols), F32),
            pltpu.VMEM((pairs + 8, 4, 128), F32),
            pltpu.VMEM((n, 12, 4, 128), F32),
            pltpu.VMEM((12, 4, 128), F32),
            pltpu.VMEM((12, 384, 512), BF16),
            pltpu.VMEM((12, NBRS, bins, 128), F32),
            pltpu.VMEM((12, bins, 128), F32),
            pltpu.VMEM((12, bins, 128), F32),
            pltpu.VMEM((2, 12, 2 * bins, 128), BF16),
            pltpu.VMEM((4, 2, 128), F32),
            pltpu.VMEM((n_lev, 4, 2, 128), F32),
            pltpu.VMEM((pairs, 2, 128), F32),
            pltpu.VMEM((8, -(-bins // 128) * 128), F32),
            pltpu.VMEM((8, -(-ent // 128) * 128), F32),
            pltpu.VMEM((6, bins, 128), F32),
            pltpu.SemaphoreType.DMA((LOADS,)),
            pltpu.SemaphoreType.DMA((2, 5)),
            pltpu.SemaphoreType.DMA((2, 5)),
            pltpu.SemaphoreType.DMA((n,)),
            pltpu.SemaphoreType.DMA((n,)),
            pltpu.SemaphoreType.DMA((n_lev,)),
            pltpu.SemaphoreType.DMA((n_lev,)),
            pltpu.SemaphoreType.DMA((n,)),
            pltpu.SemaphoreType.DMA((n,)),
        ],
        compiler_params=pltpu.CompilerParams(
            collective_id=0, has_side_effects=True, vmem_limit_bytes=56 * 1024 * 1024
        ),
    )(settle_rate, critical_stress, erosion_rate, *sources)


def solution(mesh):
    both = ("sec", "tile")
    return jax.shard_map(
        per_device,
        mesh=mesh,
        in_specs=(
            P("lev", both, None),
            P(both, None),
            P(both, None),
            P(both, None),
            P(both, None),
            P(both, None),
            P(both, None),
            P("lev"),
            P("lev"),
            P("lev"),
            P("lev", both),
            P("lev"),
            P("lev"),
            P("lev"),
            P("lev"),
            P(None, both),
            P(None, both),
            P(both),
            P(both, None),
            P(both),
            P(both),
            P(both, None, None),
        ),
        out_specs=(P("lev", both, None), P("lev", both)),
        check_vma=False,
    )
```
